256 devices in a mesh: row: 32 (over y, x, z_hi), col: 8 (over z_lo, core).
Axes of the slice: x: 4, y: 4, z: 8 (z_hi: 2, z_lo: 4; z = z_hi * 4 + z_lo), core: 2. Of those that a mesh axis runs over, the one named last changes fastest.
Arguments:
- contact_map: bfloat16 [64, 1024, 1024], P(None, 'row', 'col'), may hold values from -6 to 6
- dilations: int32 [3], replicated, may hold values from 1 to 8, as said below
- conv_weight: bfloat16 [3, 9, 32, 64], replicated, may hold values from -0.25 to 0.25
- conv_gain: float32 [3, 32], replicated, may hold values from 0.5 to 2
- conv_shift: float32 [3, 32], replicated, may hold values from -0.5 to 0.5
- out_weight: bfloat16 [3, 64, 32], replicated, may hold values from -1 to 1
Outputs:
- contact_out: bfloat16 [64, 1024, 1024], P(None, 'row', 'col')
The draws below stay inside these ranges and needn't reach their ends.
Inputs may be any that keep to these rules, and one draw needn't show every extreme that they name: `dilations`: each block's dilation; some block's dilation equals 8.
All inputs are finite; a program needn't handle non-finite values.
Results may differ from the reference program's by a relative error of at most 0.0071.
Values may be sent and summed in bfloat16 or wider, within the bound.
No kernel may reach another device: no remote copies, remote signals or barrier semaphores. Data moves between devices by JAX's collectives and lax.ppermute only.
A program may use at most 64 MiB of HBM per device.

```python
import math
import jax
import jax.numpy as jnp
from jax import lax

C = 64
HID = 32
DMAX = 8
BLOCKS = 3
BR = 32
N = 1024
N_ROW = 32


def draw_dilations(key, part):
    rate_key = jax.random.fold_in(key, 11)
    chosen_key = jax.random.fold_in(key, 23)
    dilation_rates = jax.random.randint(rate_key, (BLOCKS,), 1, DMAX + 1, dtype=jnp.int32)
    chosen = jax.random.randint(chosen_key, (), 0, BLOCKS, dtype=jnp.int32)
    positions = jnp.arange(BLOCKS, dtype=jnp.int32)
    return jnp.where(positions == chosen, DMAX, dilation_rates).astype(jnp.int32)


def shard_levels(key, extent, cuts, least, top_value):
    def one(position, parts):
        heights = jax.random.uniform(jax.random.fold_in(jax.random.fold_in(key, 6), position), (parts,), jnp.float32, least / len(cuts), top_value / len(cuts))
        return jnp.repeat(jnp.exp(heights), extent[position] // parts).reshape((-1,) + (1,) * (len(extent) - position - 1))

    loudness = one(*cuts[0])
    for cut in cuts[1:]:
        loudness = loudness * one(*cut)
    return loudness


def noise(stream_key, extent, deviation, most, shards=(), kind=jnp.bfloat16):
    result = jax.random.normal(stream_key, extent, jnp.float32) * deviation
    if len(shards) > 0:
        result = shard_levels(stream_key, extent, shards, -0.22, 0.18) * result
    return jnp.clip(result, min=-most, max=most).astype(kind)


def setup_inputs(seed: int = 0) -> dict:
    seeds = jax.random.split(jax.random.key(seed), 7)
    contact_map = noise(seeds[0], (C, N, N), 1.0, 6.0, ((1, 32), (2, 8)))
    dilations = draw_dilations(jax.random.fold_in(seeds[6], 71), 0)
    conv_weight = noise(seeds[2], (BLOCKS, 9, HID, C), (9 * C) ** -0.5, 0.25)
    conv_gain = jnp.clip(jnp.exp(jax.random.uniform(seeds[3], (BLOCKS, HID), jnp.float32, math.log(0.5), math.log(2.0))), 0.5, 2.0)
    conv_shift = jnp.clip(jax.random.uniform(seeds[4], (BLOCKS, HID), jnp.float32, -0.5, 0.5), -0.5, 0.5)
    out_weight = noise(seeds[5], (BLOCKS, C, HID), HID ** -0.5, 1.0)
    return dict(contact_map=contact_map, dilations=dilations, conv_weight=conv_weight, conv_gain=conv_gain, conv_shift=conv_shift, out_weight=out_weight)


def residual_block(feature_map, dilations, conv_weight, conv_gain, conv_shift, out_weight, layer_index):
    active = jnp.maximum(feature_map, jnp.zeros((), feature_map.dtype))
    padded = jnp.pad(active, ((0, 0), (DMAX, DMAX), (DMAX, DMAX)))
    spacing = dilations[layer_index].astype(jnp.int32)
    zero_start = jnp.zeros((), jnp.int32)
    kernel = conv_weight[layer_index].astype(jnp.float32)
    expand = out_weight[layer_index].astype(jnp.float32)
    gain_col = conv_gain[layer_index].astype(jnp.float32)[:, None, None]
    shift_col = conv_shift[layer_index].astype(jnp.float32)[:, None, None]

    def stripe(number):
        top_row = (number * BR).astype(jnp.int32)
        band_rows = lax.dynamic_slice(padded, (zero_start, top_row, zero_start), (C, BR + 2 * DMAX, N + 2 * DMAX))
        accumulated = jnp.zeros((HID, BR, N), jnp.float32)
        for offset_row in range(3):
            for offset_col in range(3):
                row_start = (DMAX + (offset_row - 1) * spacing).astype(jnp.int32)
                col_start = (DMAX + (offset_col - 1) * spacing).astype(jnp.int32)
                window = lax.dynamic_slice(band_rows, (zero_start, row_start, col_start), (C, BR, N))
                accumulated = accumulated + jnp.einsum("oc,cyx->oyx", kernel[3 * offset_row + offset_col], window.astype(jnp.float32))
        hidden = jnp.maximum(gain_col * accumulated + shift_col, 0.0).astype(jnp.bfloat16)
        center = lax.dynamic_slice(feature_map, (zero_start, top_row, zero_start), (C, BR, N))
        updated = center.astype(jnp.float32) + jnp.einsum("oh,hyx->oyx", expand, hidden.astype(jnp.float32))
        return updated.astype(jnp.bfloat16)

    stripes = lax.map(stripe, jnp.arange(N_ROW, dtype=jnp.int32))
    return jnp.transpose(stripes, (1, 0, 2, 3)).reshape(C, N, N)


def reference(contact_map, dilations, conv_weight, conv_gain, conv_shift, out_weight):
    feature_map = contact_map
    for layer_index in range(BLOCKS):
        if layer_index == 2:
            mirrored = jnp.swapaxes(feature_map, 1, 2)
            feature_map = (0.5 * (feature_map.astype(jnp.float32) + mirrored.astype(jnp.float32))).astype(jnp.bfloat16)
        feature_map = residual_block(feature_map, dilations, conv_weight, conv_gain, conv_shift, out_weight, layer_index)
    return feature_map
```

```python
import functools

import jax
import jax.numpy as jnp
from jax import lax
from jax.experimental import pallas as pl
from jax.experimental.pallas import tpu as pltpu
from jax.sharding import PartitionSpec as P

D = 8
BOTH = ("row", "col")
BF = jnp.bfloat16
F32 = jnp.float32
VMEM = pl.BlockSpec(memory_space=pltpu.VMEM)
SMEM = pl.BlockSpec(memory_space=pltpu.SMEM)
LIMIT = 40 * 1024 * 1024


def call(body, outs, args, n_smem, scratch, flops, moved):
    return pl.pallas_call(
        body,
        out_shape=outs,
        in_specs=[SMEM] * n_smem + [VMEM] * (len(args) - n_smem),
        out_specs=jax.tree.map(lambda _: VMEM, outs),
        scratch_shapes=scratch,
        compiler_params=pltpu.CompilerParams(vmem_limit_bytes=LIMIT),
        cost_estimate=pl.CostEstimate(flops=flops, bytes_accessed=moved, transcendentals=0),
    )(*args)


def lanes(rows):
    return lax.broadcasted_iota(jnp.int32, (rows, 128), 1)


def pack_strips(pieces, start, width, count):
    lane = lanes(64)
    total = None
    for place, piece in enumerate(pieces):
        moved = pltpu.roll(piece.astype(F32), (place * width - start) % 128, 1)
        total = moved if total is None else jnp.where(lane >= place * width, moved, total)
    return total.astype(BF)


def side_lanes(from_right, from_left, place, width):
    lane = lanes(64)
    right = pltpu.roll(from_right.astype(F32), (-place * width) % 128, 1)
    left = pltpu.roll(from_left.astype(F32), (128 - width - place * width) % 128, 1)
    side = jnp.where(lane < width, right, jnp.where(lane >= 128 - width, left, 0.0))
    return side.astype(BF)


def block_row(source, at, spacing, kernel, gain, shift, expand):
    stacked = jnp.concatenate(
        [source[at - spacing], source[at], source[at + spacing]], axis=0
    )
    taps = jnp.dot(kernel, jnp.maximum(stacked, 0), preferred_element_type=F32)
    conv = (
        taps[32:64]
        + pltpu.roll(taps[:32], spacing, 1)
        + pltpu.roll(taps[64:], 256 - spacing, 1)
    )
    hidden = jnp.maximum(gain * conv + shift, 0.0).astype(BF)
    return source[at].astype(F32) + jnp.dot(expand, hidden, preferred_element_type=F32)


def pack_first(up_ref, own_ref, down_ref, left_ref, right_ref):
    def step(g, _):
        pieces = [up_ref[g], own_ref[g], own_ref[g + 16], down_ref[g]]
        left_ref[g] = pack_strips(pieces, 0, 32, 4)
        right_ref[g] = pack_strips(pieces, 96, 32, 4)
        return _

    lax.fori_loop(0, 16, step, 0)


def first_blocks(
    spacing_ref, place_ref, up_ref, own_ref, down_ref, from_left, from_right,
    kernel_ref, gain_ref, shift_ref, expand_ref,
    center_ref, message_ref, wide, middle, turned, pair,
):
    row, col = place_ref[0], place_ref[1]
    members = place_ref[2]

    def fill(g, _):
        for q, ref in enumerate((up_ref, own_ref, own_ref, down_ref)):
            wide[q * 16 + g, :, :128] = ref[g + (16 if q == 2 else 0)]
            wide[q * 16 + g, :, 128:] = side_lanes(from_right[g], from_left[g], q, 32)
        return _

    lax.fori_loop(0, 16, fill, 0)
    lane = lax.broadcasted_iota(jnp.int32, (64, 256), 1)
    inside = (lane < 128) | ((lane < 192) & (col < 7)) | ((lane >= 192) & (col > 0))

    def one(r, _):
        out = block_row(
            wide, r + 8, spacing_ref[0], kernel_ref[0], gain_ref[0], shift_ref[0], expand_ref[0]
        )
        number = 32 * row - 8 + r
        alive = inside & (number >= 0) & (number < 1024)
        middle[r] = jnp.where(alive, out, 0.0).astype(BF)
        return _

    lax.fori_loop(0, 48, one, 0, unroll=4)

    def two(i, _):
        for half in range(2):
            r = i + 16 * half
            out = block_row(
                middle, r + 8, spacing_ref[1], kernel_ref[1], gain_ref[1], shift_ref[1],
                expand_ref[1],
            )
            out = jnp.where(inside, out, 0.0).astype(BF)
            center_ref[r] = out[:, :128]
            pair[64 * half : 64 * half + 64] = pltpu.roll(out.astype(F32), 8, 1)
        across = jnp.transpose(pair[...])
        turned[pl.ds(i, 144, stride=16), :] = across[:144]
        return _

    lax.fori_loop(0, 16, two, 0, unroll=2)
    for m in range(4):
        message_ref[lax.rem(m - members + 4, 4)] = turned[
            512 * m : 512 * m + 768
        ].astype(BF)


def average(
    place_ref, center_ref, up_ref, down_ref, m0, m1, m2, m3,
    mean_ref, left_ref, right_ref, gathered,
):
    members = place_ref[2]
    for t, ref in enumerate((m0, m1, m2, m3)):
        gathered[lax.rem(members - t + 4, 4)] = ref[...]

    def step(j, mine):
        blocks = []
        start = pl.multiple_of(j * 16, 16)
        for k in range(4):
            part = gathered[k, pl.ds(start, 16), :].astype(F32)
            blocks += [part, pltpu.roll(part, 64, 1)]
        mirrored = jnp.transpose(jnp.concatenate(blocks, axis=0))[:64]
        mean_ref[j] = (0.5 * (mine.astype(F32) + mirrored)).astype(BF)

    def above(j, _):
        step(j, up_ref[j])
        return _

    def inner(j, _):
        step(j + 8, center_ref[j])
        return _

    def below(j, _):
        step(j + 40, down_ref[j])
        return _

    lax.fori_loop(0, 8, above, 0, unroll=2)
    lax.fori_loop(0, 32, inner, 0, unroll=2)
    lax.fori_loop(0, 8, below, 0, unroll=2)

    def strips(g, _):
        pieces = [mean_ref[8 * g + q] for q in range(8)]
        left_ref[g] = pack_strips(pieces, 0, 16, 8)
        right_ref[g] = pack_strips(pieces, 112, 16, 8)
        return _

    lax.fori_loop(0, 6, strips, 0)


def last_block(
    spacing_ref, mean_ref, from_left, from_right, kernel_ref, gain_ref, shift_ref, expand_ref,
    out_ref, wide,
):
    def fill(g, _):
        for q in range(8):
            wide[8 * g + q, :, :128] = mean_ref[8 * g + q]
            wide[8 * g + q, :, 128:] = side_lanes(from_right[g], from_left[g], q, 16)
        return _

    lax.fori_loop(0, 6, fill, 0)

    def one(r, _):
        out = block_row(
            wide, r + 8, spacing_ref[2], kernel_ref[2], gain_ref[2], shift_ref[2], expand_ref[2]
        )
        out_ref[r] = out[:, :128].astype(BF)
        return _

    lax.fori_loop(0, 32, one, 0, unroll=4)


def on_device(contact_map, dilations, conv_weight, conv_gain, conv_shift, out_weight):
    rows, cols = lax.axis_size("row"), lax.axis_size("col")
    row, col = lax.axis_index("row"), lax.axis_index("col")
    place = jnp.stack([row, col, lax.rem(row, 4)]).astype(jnp.int32)
    down_way = [(r, r + 1) for r in range(rows - 1)]
    up_way = [(r + 1, r) for r in range(rows - 1)]
    right_way = [(c, c + 1) for c in range(cols - 1)]
    left_way = [(c + 1, c) for c in range(cols - 1)]

    own = jnp.transpose(contact_map, (1, 0, 2))
    above = lax.ppermute(own[16:], "row", down_way)
    below = lax.ppermute(own[:16], "row", up_way)
    kernel = jnp.transpose(conv_weight.reshape(3, 3, 3, 32, 64), (0, 2, 3, 1, 4)).reshape(3, 96, 192)
    gain = jnp.broadcast_to(conv_gain[:, :, None], (3, 32, 256))
    shift = jnp.broadcast_to(conv_shift[:, :, None], (3, 32, 256))
    weights = (kernel, gain, shift, out_weight)

    strip = jax.ShapeDtypeStruct((16, 64, 128), BF)
    to_left, to_right = call(
        pack_first, (strip, strip), (above, own, below), 0, [], 0, 2 << 20
    )
    from_left = lax.ppermute(to_right, "col", right_way)
    from_right = lax.ppermute(to_left, "col", left_way)

    center, messages = call(
        first_blocks,
        (jax.ShapeDtypeStruct((32, 64, 128), BF), jax.ShapeDtypeStruct((4, 768, 128), BF)),
        (dilations, place, above, own, below, from_left, from_right, *weights),
        2,
        [
            pltpu.VMEM((64, 64, 256), BF),
            pltpu.VMEM((48, 64, 256), BF),
            pltpu.VMEM((144 * 16, 128), F32),
            pltpu.VMEM((128, 256), F32),
        ],
        80 * 256 * 64 * 32 * 20,
        4 << 20,
    )
    above = lax.ppermute(center[24:], "row", down_way)
    below = lax.ppermute(center[:8], "row", up_way)
    received = []
    for t in range(4):
        pairs = []
        for a in range(rows // 4):
            for k in range(4):
                for b in range(cols):
                    pairs.append(((4 * a + k) * cols + b, (4 * b + (k + t) % 4) * cols + a))
        received.append(lax.ppermute(messages[t], BOTH, pairs))

    strip = jax.ShapeDtypeStruct((6, 64, 128), BF)
    mean, to_left, to_right = call(
        average,
        (jax.ShapeDtypeStruct((48, 64, 128), BF), strip, strip),
        (place, center, above, below, *received),
        1,
        [pltpu.VMEM((4, 768, 128), BF)],
        0,
        3 << 20,
    )
    from_left = lax.ppermute(to_right, "col", right_way)
    from_right = lax.ppermute(to_left, "col", left_way)
    out = call(
        last_block,
        jax.ShapeDtypeStruct((32, 64, 128), BF),
        (dilations, mean, from_left, from_right, *weights),
        1,
        [pltpu.VMEM((48, 64, 256), BF)],
        32 * 256 * 64 * 32 * 20,
        2 << 20,
    )
    return jnp.transpose(out, (1, 0, 2))


def solution(mesh):
    return jax.shard_map(
        on_device,
        mesh=mesh,
        in_specs=(P(None, "row", "col"), P(), P(), P(), P(), P()),
        out_specs=P(None, "row", "col"),
        check_vma=False,
    )
```

```python
import functools

import jax
import jax.numpy as jnp
from jax import lax
from jax.experimental import pallas as pl
from jax.experimental.pallas import tpu as pltpu
from jax.sharding import PartitionSpec as P

D = 8
BOTH = ("row", "col")
BF = jnp.bfloat16
F32 = jnp.float32
VMEM = pl.BlockSpec(memory_space=pltpu.VMEM)
SMEM = pl.BlockSpec(memory_space=pltpu.SMEM)
LIMIT = 40 * 1024 * 1024


def call(body, outs, args, n_smem, scratch, flops, moved):
    return pl.pallas_call(
        body,
        out_shape=outs,
        in_specs=[SMEM] * n_smem + [VMEM] * (len(args) - n_smem),
        out_specs=jax.tree.map(lambda _: VMEM, outs),
        scratch_shapes=scratch,
        compiler_params=pltpu.CompilerParams(vmem_limit_bytes=LIMIT),
        cost_estimate=pl.CostEstimate(flops=flops, bytes_accessed=moved, transcendentals=0),
    )(*args)


def lanes(rows):
    return lax.broadcasted_iota(jnp.int32, (rows, 128), 1)


def pack_strips(pieces, start, width):
    lane = lanes(64)
    total = None
    for place, piece in enumerate(pieces):
        moved = pltpu.roll(piece.astype(F32), (place * width - start) % 128, 1)
        total = moved if total is None else jnp.where(lane >= place * width, moved, total)
    return total.astype(BF)


def side_lanes(from_right, from_left, place, width):
    lane = lanes(64)
    right = pltpu.roll(from_right.astype(F32), (-place * width) % 128, 1)
    left = pltpu.roll(from_left.astype(F32), (128 - width - place * width) % 128, 1)
    side = jnp.where(lane < width, right, jnp.where(lane >= 128 - width, left, 0.0))
    return side.astype(BF)


def block_rows(source, rows, spacing, kernel, gain, shift, expand, narrow=False):
    taps = []
    for at in rows:
        stacked = jnp.concatenate(
            [source[at - spacing], source[at], source[at + spacing]], axis=0
        )
        taps.append(jnp.dot(kernel, jnp.maximum(stacked, 0), preferred_element_type=F32))
    lane = lanes(32)
    before, after = lane >= spacing, lane < 128 - spacing
    hidden = []
    for tap in taps:
        left = [pltpu.roll(tap[:32, h : h + 128], spacing, 1) for h in (0, 128)]
        right = [pltpu.roll(tap[64:, h : h + 128], 128 - spacing, 1) for h in (0, 128)]
        convs = []
        for h in range(1 if narrow else 2):
            convs.append(
                tap[32:64, 128 * h : 128 * h + 128]
                + jnp.where(before, left[h], left[1 - h])
                + jnp.where(after, right[h], right[1 - h])
            )
        hidden.append(
            [jnp.maximum(gain * conv + shift, 0.0).astype(BF) for conv in convs]
        )
    if narrow:
        hidden = [[h[0] for h in hidden[i : i + 2]] for i in range(0, len(rows), 2)]
    grown = [
        jnp.dot(expand, jnp.concatenate(h, axis=1), preferred_element_type=F32) for h in hidden
    ]
    if narrow:
        halves = [g[:, h : h + 128] for g in grown for h in (0, 128)]
        return [source[at, :, :128].astype(F32) + half for at, half in zip(rows, halves)]
    return [source[at].astype(F32) + g for at, g in zip(rows, grown)]


def block_of(layer, spacing_ref, kernel_ref, gain_ref, shift_ref, expand_ref):
    return (
        spacing_ref[layer], kernel_ref[layer], gain_ref[layer], shift_ref[layer], expand_ref[layer]
    )


def pack_first(up_ref, own_ref, down_ref, left_ref, right_ref):
    for ref, groups, first in ((up_ref, 6, 0), (own_ref, 8, 6), (down_ref, 6, 14)):

        def step(g, _):
            pieces = [ref[4 * g + q] for q in range(4)]
            left_ref[first + g] = pack_strips(pieces, 0, 32)
            right_ref[first + g] = pack_strips(pieces, 96, 32)
            return _

        lax.fori_loop(0, groups, step, 0, unroll=groups)


def first_blocks(
    spacing_ref, place_ref, up_ref, own_ref, down_ref, from_left, from_right,
    kernel_ref, gain_ref, shift_ref, expand_ref,
    center_ref, message_ref, wide, middle, turned,
):
    row, col = place_ref[0], place_ref[1]
    members = place_ref[2]
    weights = (spacing_ref, kernel_ref, gain_ref, shift_ref, expand_ref)

    for ref, groups, first in ((up_ref, 6, 0), (own_ref, 8, 6), (down_ref, 6, 14)):

        def fill(g, _):
            for q in range(4):
                at = 4 * (g + first) + q
                wide[at, :, :128] = ref[4 * g + q]
                wide[at, :, 128:] = side_lanes(
                    from_right[first + g], from_left[first + g], q, 32
                )
            return _

        lax.fori_loop(0, groups, fill, 0, unroll=2)
    lane = lax.broadcasted_iota(jnp.int32, (64, 256), 1)
    inside = (lane < 128) | ((lane < 192) & (col < 7)) | ((lane >= 192) & (col > 0))

    def kept(out, number):
        alive = inside & (number >= 0) & (number < 1024)
        return jnp.where(alive, out, 0.0)

    def one(i, _):
        start = i * 32
        outs = block_rows(wide, [start + b + 8 for b in range(32)], *block_of(0, *weights))
        for b, out in enumerate(outs):
            middle[start + b] = kept(out, 32 * row - 16 + start + b).astype(BF)
        return _

    lax.fori_loop(0, 2, one, 0)

    def two(i, _):
        start = i * 8
        rows = [40 * i + b for b in range(8)]
        for b in range(8):
            rows += [8 + start + b, 24 + start + b]
        outs = block_rows(middle, [r + 8 for r in rows], *block_of(1, *weights))
        outs = [kept(out, 32 * row - 8 + r) for r, out in zip(rows, outs)]
        for r, out in zip(rows, outs):
            center_ref[r] = out[:, :128].astype(BF)
        for b in range(8):
            pair = jnp.concatenate(outs[8 + 2 * b : 10 + 2 * b], axis=0).astype(BF)
            across = jnp.transpose(pltpu.roll(pair.astype(F32), 8, 1))
            turned[pl.ds(start + b, 144, stride=16), :] = across[:144]
        return _

    lax.fori_loop(0, 2, two, 0)
    for m in range(4):
        message_ref[lax.rem(m - members + 4, 4)] = turned[512 * m : 512 * m + 768].astype(BF)


def average(
    place_ref, center_ref, m0, m1, m2, m3, mean_ref, left_ref, right_ref, gathered
):
    members = place_ref[2]
    for t, ref in enumerate((m0, m1, m2, m3)):
        gathered[lax.rem(members - t + 4, 4)] = ref[...]

    def step(j, _):
        blocks = []
        start = pl.multiple_of(j * 16, 16)
        for k in range(4):
            part = gathered[k, pl.ds(start, 16), :].astype(F32)
            blocks += [part, pltpu.roll(part, 64, 1)]
        mirrored = jnp.transpose(jnp.concatenate(blocks, axis=0))[:64]
        mean_ref[j] = (0.5 * (center_ref[j].astype(F32) + mirrored)).astype(BF)
        return _

    lax.fori_loop(0, 48, step, 0, unroll=8)
    for g in range(6):
        pieces = [mean_ref[8 * g + q] for q in range(8)]
        left_ref[g] = pack_strips(pieces, 0, 16)
        right_ref[g] = pack_strips(pieces, 112, 16)


def last_block(
    spacing_ref, mean_ref, from_left, from_right, kernel_ref, gain_ref, shift_ref, expand_ref,
    out_ref, wide,
):
    weights = (spacing_ref, kernel_ref, gain_ref, shift_ref, expand_ref)
    for g in range(6):
        for q in range(8):
            wide[8 * g + q, :, :128] = mean_ref[8 * g + q]
            wide[8 * g + q, :, 128:] = side_lanes(from_right[g], from_left[g], q, 16)
    outs = block_rows(wide, [r + 8 for r in range(32)], *block_of(2, *weights), narrow=True)
    for r, out in enumerate(outs):
        out_ref[r] = out.astype(BF)


def on_device(contact_map, dilations, conv_weight, conv_gain, conv_shift, out_weight):
    rows, cols = lax.axis_size("row"), lax.axis_size("col")
    row, col = lax.axis_index("row"), lax.axis_index("col")
    place = jnp.stack([row, col, lax.rem(row, 4)]).astype(jnp.int32)
    down_way = [(r, r + 1) for r in range(rows - 1)]
    up_way = [(r + 1, r) for r in range(rows - 1)]
    right_way = [(c, c + 1) for c in range(cols - 1)]
    left_way = [(c + 1, c) for c in range(cols - 1)]

    own = jnp.transpose(contact_map, (1, 0, 2))
    above = lax.ppermute(own[8:], "row", down_way)
    below = lax.ppermute(own[:24], "row", up_way)
    kernel = jnp.transpose(conv_weight.reshape(3, 3, 3, 32, 64), (0, 2, 3, 1, 4)).reshape(3, 96, 192)
    gain = jnp.broadcast_to(conv_gain[:, :, None], (3, 32, 128))
    shift = jnp.broadcast_to(conv_shift[:, :, None], (3, 32, 128))
    weights = (kernel, gain, shift, out_weight)

    strip = jax.ShapeDtypeStruct((20, 64, 128), BF)
    to_left, to_right = call(
        pack_first, (strip, strip), (above, own, below), 0, [], 0, 2 << 20
    )
    from_left = lax.ppermute(to_right, "col", right_way)
    from_right = lax.ppermute(to_left, "col", left_way)

    center, messages = call(
        first_blocks,
        (jax.ShapeDtypeStruct((48, 64, 128), BF), jax.ShapeDtypeStruct((4, 768, 128), BF)),
        (dilations, place, above, own, below, from_left, from_right, *weights),
        2,
        [
            pltpu.VMEM((80, 64, 256), BF),
            pltpu.VMEM((64, 64, 256), BF),
            pltpu.VMEM((144 * 16, 128), F32),
        ],
        112 * 256 * 64 * 32 * 20,
        4 << 20,
    )
    received = []
    for t in range(4):
        pairs = []
        for a in range(rows // 4):
            for k in range(4):
                for b in range(cols):
                    pairs.append(((4 * a + k) * cols + b, (4 * b + (k + t) % 4) * cols + a))
        received.append(lax.ppermute(messages[t], BOTH, pairs))

    strip = jax.ShapeDtypeStruct((6, 64, 128), BF)
    mean, to_left, to_right = call(
        average,
        (jax.ShapeDtypeStruct((48, 64, 128), BF), strip, strip),
        (place, center, *received),
        1,
        [pltpu.VMEM((4, 768, 128), BF)],
        0,
        3 << 20,
    )
    from_left = lax.ppermute(to_right, "col", right_way)
    from_right = lax.ppermute(to_left, "col", left_way)
    out = call(
        last_block,
        jax.ShapeDtypeStruct((32, 64, 128), BF),
        (dilations, mean, from_left, from_right, *weights),
        1,
        [pltpu.VMEM((48, 64, 256), BF)],
        32 * 256 * 64 * 32 * 20,
        2 << 20,
    )
    return jnp.transpose(out, (1, 0, 2))


def solution(mesh):
    return jax.shard_map(
        on_device,
        mesh=mesh,
        in_specs=(P(None, "row", "col"), P(), P(), P(), P(), P()),
        out_specs=P(None, "row", "col"),
        check_vma=False,
    )
```

```python
import functools

import jax
import jax.numpy as jnp
from jax import lax
from jax.experimental import pallas as pl
from jax.experimental.pallas import tpu as pltpu
from jax.sharding import PartitionSpec as P

D = 8
BOTH = ("row", "col")
BF = jnp.bfloat16
F32 = jnp.float32
VMEM = pl.BlockSpec(memory_space=pltpu.VMEM)
SMEM = pl.BlockSpec(memory_space=pltpu.SMEM)
LIMIT = 40 * 1024 * 1024


def call(body, outs, args, n_smem, scratch, flops, moved):
    return pl.pallas_call(
        body,
        out_shape=outs,
        in_specs=[SMEM] * n_smem + [VMEM] * (len(args) - n_smem),
        out_specs=jax.tree.map(lambda _: VMEM, outs),
        scratch_shapes=scratch,
        compiler_params=pltpu.CompilerParams(vmem_limit_bytes=LIMIT),
        cost_estimate=pl.CostEstimate(flops=flops, bytes_accessed=moved, transcendentals=0),
    )(*args)


def lanes(rows):
    return lax.broadcasted_iota(jnp.int32, (rows, 128), 1)


def pack_strips(pieces, start, width):
    lane = lanes(64)
    total = None
    for place, piece in enumerate(pieces):
        moved = pltpu.roll(piece.astype(F32), (place * width - start) % 128, 1)
        total = moved if total is None else jnp.where(lane >= place * width, moved, total)
    return total.astype(BF)


def side_lanes(from_right, from_left, place, width):
    lane = lanes(64)
    right = pltpu.roll(from_right.astype(F32), (-place * width) % 128, 1)
    left = pltpu.roll(from_left.astype(F32), (128 - width - place * width) % 128, 1)
    side = jnp.where(lane < width, right, jnp.where(lane >= 128 - width, left, 0.0))
    return side.astype(BF)


def block_rows(source, rows, spacing, kernel, gain, shift, expand, narrow=False):
    taps = []
    for at in rows:
        stacked = jnp.concatenate(
            [source[at - spacing], source[at], source[at + spacing]], axis=0
        )
        taps.append(jnp.dot(kernel, jnp.maximum(stacked, 0), preferred_element_type=F32))
    lane = lanes(32)
    before, after = lane >= spacing, lane < 128 - spacing
    hidden = []
    for tap in taps:
        left = [pltpu.roll(tap[:32, h : h + 128], spacing, 1) for h in (0, 128)]
        right = [pltpu.roll(tap[64:, h : h + 128], 128 - spacing, 1) for h in (0, 128)]
        convs = []
        for h in range(1 if narrow else 2):
            convs.append(
                tap[32:64, 128 * h : 128 * h + 128]
                + jnp.where(before, left[h], left[1 - h])
                + jnp.where(after, right[h], right[1 - h])
            )
        hidden.append(
            [jnp.maximum(gain * conv + shift, 0.0).astype(BF) for conv in convs]
        )
    if narrow:
        hidden = [[h[0] for h in hidden[i : i + 2]] for i in range(0, len(rows), 2)]
    grown = [
        jnp.dot(expand, jnp.concatenate(h, axis=1), preferred_element_type=F32) for h in hidden
    ]
    if narrow:
        halves = [g[:, h : h + 128] for g in grown for h in (0, 128)]
        return [source[at, :, :128].astype(F32) + half for at, half in zip(rows, halves)]
    return [source[at].astype(F32) + g for at, g in zip(rows, grown)]


def block_of(layer, spacing_ref, kernel_ref, gain_ref, shift_ref, expand_ref):
    return (
        spacing_ref[layer], kernel_ref[layer], gain_ref[layer], shift_ref[layer], expand_ref[layer]
    )


def pack_sides(up_ref, own_ref, down_ref, left_ref, right_ref):
    first = 0
    for ref in (up_ref, own_ref, down_ref):
        for g in range(ref.shape[0] // 8):
            pieces = [ref[8 * g + q] for q in range(8)]
            left_ref[first + g] = pack_strips(pieces, 0, 16)
            right_ref[first + g] = pack_strips(pieces, 112, 16)
        first += ref.shape[0] // 8


def fill_wide(wide, up_ref, own_ref, down_ref, from_left, from_right):
    first = 0
    for ref in (up_ref, own_ref, down_ref):
        for r in range(ref.shape[0]):
            at = first + r
            wide[at, :, :128] = ref[r]
            wide[at, :, 128:] = side_lanes(from_right[at // 8], from_left[at // 8], at % 8, 16)
        first += ref.shape[0]


def first_blocks(
    spacing_ref, place_ref, up_ref, own_ref, down_ref, from_left, from_right,
    kernel_ref, gain_ref, shift_ref, expand_ref,
    second_ref, message_ref, wide, middle, turned,
):
    row, col = place_ref[0], place_ref[1]
    members = place_ref[2]
    weights = (spacing_ref, kernel_ref, gain_ref, shift_ref, expand_ref)
    fill_wide(wide, up_ref, own_ref, down_ref, from_left, from_right)
    lane = lax.broadcasted_iota(jnp.int32, (64, 256), 1)
    inside = (lane < 128) | ((lane < 192) & (col < 7)) | ((lane >= 192) & (col > 0))

    def one(i, _):
        start = i * 24
        outs = block_rows(wide, [start + b + 8 for b in range(24)], *block_of(0, *weights))
        for b, out in enumerate(outs):
            number = 32 * row - 8 + start + b
            alive = inside & (number >= 0) & (number < 1024)
            middle[start + b] = jnp.where(alive, out, 0.0).astype(BF)
        return _

    lax.fori_loop(0, 2, one, 0)
    rows = [r for b in range(16) for r in (b, b + 16)]
    outs = block_rows(middle, [r + 8 for r in rows], *block_of(1, *weights), narrow=True)
    for r, out in zip(rows, outs):
        second_ref[r] = out.astype(BF)
    for b in range(16):
        pair = jnp.concatenate(outs[2 * b : 2 * b + 2], axis=0).astype(BF)
        turned[pl.ds(b, 128, stride=16), :] = jnp.transpose(pair.astype(F32))
    for m in range(4):
        message_ref[lax.rem(m - members + 4, 4)] = turned[512 * m : 512 * m + 512].astype(BF)


def average(place_ref, second_ref, m0, m1, m2, m3, mean_ref, gathered):
    members = place_ref[2]
    for t, ref in enumerate((m0, m1, m2, m3)):
        gathered[lax.rem(members - t + 4, 4)] = ref[...]
    for j in range(32):
        blocks = []
        for k in range(4):
            part = gathered[k, 16 * j : 16 * j + 16, :].astype(F32)
            blocks += [part, pltpu.roll(part, 64, 1)]
        mirrored = jnp.transpose(jnp.concatenate(blocks, axis=0))[:64]
        mean_ref[j] = (0.5 * (second_ref[j].astype(F32) + mirrored)).astype(BF)


def last_block(
    spacing_ref, up_ref, own_ref, down_ref, from_left, from_right,
    kernel_ref, gain_ref, shift_ref, expand_ref, out_ref, wide,
):
    weights = (spacing_ref, kernel_ref, gain_ref, shift_ref, expand_ref)
    fill_wide(wide, up_ref, own_ref, down_ref, from_left, from_right)
    outs = block_rows(wide, [r + 8 for r in range(32)], *block_of(2, *weights), narrow=True)
    for r, out in enumerate(outs):
        out_ref[r] = out.astype(BF)


def on_device(contact_map, dilations, conv_weight, conv_gain, conv_shift, out_weight):
    rows, cols = lax.axis_size("row"), lax.axis_size("col")
    row, col = lax.axis_index("row"), lax.axis_index("col")
    place = jnp.stack([row, col, lax.rem(row, 4)]).astype(jnp.int32)
    down_way = [(r, r + 1) for r in range(rows - 1)]
    up_way = [(r + 1, r) for r in range(rows - 1)]
    right_way = [(c, c + 1) for c in range(cols - 1)]
    left_way = [(c + 1, c) for c in range(cols - 1)]

    def rims(own, depth):
        above = lax.ppermute(own[32 - depth :], "row", down_way)
        below = lax.ppermute(own[:depth], "row", up_way)
        strip = jax.ShapeDtypeStruct(((32 + 2 * depth) // 8, 64, 128), BF)
        to_left, to_right = call(
            pack_sides, (strip, strip), (above, own, below), 0, [], 0, 1 << 20
        )
        from_left = lax.ppermute(to_right, "col", right_way)
        from_right = lax.ppermute(to_left, "col", left_way)
        return above, own, below, from_left, from_right

    own = jnp.transpose(contact_map, (1, 0, 2))
    kernel = jnp.transpose(conv_weight.reshape(3, 3, 3, 32, 64), (0, 2, 3, 1, 4)).reshape(3, 96, 192)
    gain = jnp.broadcast_to(conv_gain[:, :, None], (3, 32, 128))
    shift = jnp.broadcast_to(conv_shift[:, :, None], (3, 32, 128))
    weights = (kernel, gain, shift, out_weight)

    tile = jax.ShapeDtypeStruct((32, 64, 128), BF)
    second, messages = call(
        first_blocks,
        (tile, jax.ShapeDtypeStruct((4, 512, 128), BF)),
        (dilations, place, *rims(own, 16), *weights),
        2,
        [
            pltpu.VMEM((64, 64, 256), BF),
            pltpu.VMEM((48, 64, 256), BF),
            pltpu.VMEM((128 * 16, 128), F32),
        ],
        80 * 256 * 64 * 32 * 20,
        4 << 20,
    )
    received = []
    for t in range(4):
        pairs = []
        for a in range(rows // 4):
            for k in range(4):
                for b in range(cols):
                    pairs.append(((4 * a + k) * cols + b, (4 * b + (k + t) % 4) * cols + a))
        received.append(lax.ppermute(messages[t], BOTH, pairs))
    mean = call(
        average,
        tile,
        (place, second, *received),
        1,
        [pltpu.VMEM((4, 512, 128), BF)],
        0,
        2 << 20,
    )
    out = call(
        last_block,
        tile,
        (dilations, *rims(mean, 8), *weights),
        1,
        [pltpu.VMEM((48, 64, 256), BF)],
        32 * 256 * 64 * 32 * 20,
        2 << 20,
    )
    return jnp.transpose(out, (1, 0, 2))


def solution(mesh):
    return jax.shard_map(
        on_device,
        mesh=mesh,
        in_specs=(P(None, "row", "col"), P(), P(), P(), P(), P()),
        out_specs=P(None, "row", "col"),
        check_vma=False,
    )
```

```python
import functools

import jax
import jax.numpy as jnp
from jax import lax
from jax.experimental import pallas as pl
from jax.experimental.pallas import tpu as pltpu
from jax.sharding import PartitionSpec as P

D = 8
BOTH = ("row", "col")
BF = jnp.bfloat16
F32 = jnp.float32
VMEM = pl.BlockSpec(memory_space=pltpu.VMEM)
SMEM = pl.BlockSpec(memory_space=pltpu.SMEM)
LIMIT = 40 * 1024 * 1024


def call(body, outs, args, n_smem, scratch, flops, moved):
    return pl.pallas_call(
        body,
        out_shape=outs,
        in_specs=[SMEM] * n_smem + [VMEM] * (len(args) - n_smem),
        out_specs=jax.tree.map(lambda _: VMEM, outs),
        scratch_shapes=scratch,
        compiler_params=pltpu.CompilerParams(vmem_limit_bytes=LIMIT),
        cost_estimate=pl.CostEstimate(flops=flops, bytes_accessed=moved, transcendentals=0),
    )(*args)


def lanes(rows):
    return lax.broadcasted_iota(jnp.int32, (rows, 128), 1)


def pack_strips(pieces, start, width):
    lane = lanes(64)
    total = None
    for place, piece in enumerate(pieces):
        moved = pltpu.roll(piece.astype(F32), (place * width - start) % 128, 1)
        total = moved if total is None else jnp.where(lane >= place * width, moved, total)
    return total.astype(BF)


def side_lanes(from_right, from_left, place, width):
    lane = lanes(64)
    right = pltpu.roll(from_right.astype(F32), (-place * width) % 128, 1)
    left = pltpu.roll(from_left.astype(F32), (128 - width - place * width) % 128, 1)
    side = jnp.where(lane < width, right, jnp.where(lane >= 128 - width, left, 0.0))
    return side.astype(BF)


def block_rows(source, rows, spacing, kernel, gain, shift, expand, narrow=False):
    taps = []
    for at in rows:
        stacked = jnp.concatenate(
            [source[at - spacing], source[at], source[at + spacing]], axis=0
        )
        taps.append(jnp.dot(kernel, jnp.maximum(stacked, 0), preferred_element_type=F32))
    lane = lanes(32)
    before, after = lane >= spacing, lane < 128 - spacing
    hidden = []
    for tap in taps:
        left = [pltpu.roll(tap[:32, h : h + 128], spacing, 1) for h in (0, 128)]
        right = [pltpu.roll(tap[64:, h : h + 128], 128 - spacing, 1) for h in (0, 128)]
        convs = []
        for h in range(1 if narrow else 2):
            convs.append(
                tap[32:64, 128 * h : 128 * h + 128]
                + jnp.where(before, left[h], left[1 - h])
                + jnp.where(after, right[h], right[1 - h])
            )
        hidden.append(
            [jnp.maximum(gain * conv + shift, 0.0).astype(BF) for conv in convs]
        )
    if narrow:
        hidden = [[h[0] for h in hidden[i : i + 2]] for i in range(0, len(rows), 2)]
    grown = [
        jnp.dot(expand, jnp.concatenate(h, axis=1), preferred_element_type=F32) for h in hidden
    ]
    if narrow:
        halves = [g[:, h : h + 128] for g in grown for h in (0, 128)]
        return [source[at, :, :128].astype(F32) + half for at, half in zip(rows, halves)]
    return [source[at].astype(F32) + g for at, g in zip(rows, grown)]


def block_of(layer, spacing_ref, kernel_ref, gain_ref, shift_ref, expand_ref):
    return (
        spacing_ref[layer], kernel_ref[layer], gain_ref[layer], shift_ref[layer], expand_ref[layer]
    )


def pack_sides(up_ref, own_ref, down_ref, left_ref, right_ref):
    first = 0
    for ref in (up_ref, own_ref, down_ref):
        for g in range(ref.shape[0] // 8):
            pieces = [ref[8 * g + q] for q in range(8)]
            left_ref[first + g] = pack_strips(pieces, 0, 16)
            right_ref[first + g] = pack_strips(pieces, 112, 16)
        first += ref.shape[0] // 8


def fill_wide(wide, up_ref, own_ref, down_ref, from_left, from_right):
    first = 0
    for ref in (up_ref, own_ref, down_ref):
        for r in range(ref.shape[0]):
            at = first + r
            wide[at, :, :128] = ref[r]
            wide[at, :, 128:] = side_lanes(from_right[at // 8], from_left[at // 8], at % 8, 16)
        first += ref.shape[0]


def first_blocks(
    spacing_ref, place_ref, up_ref, own_ref, down_ref, from_left, from_right,
    kernel_ref, gain_ref, shift_ref, expand_ref,
    second_ref, message_ref, wide, middle, turned,
):
    row, col = place_ref[0], place_ref[1]
    members = place_ref[2]
    weights = (spacing_ref, kernel_ref, gain_ref, shift_ref, expand_ref)
    fill_wide(wide, up_ref, own_ref, down_ref, from_left, from_right)
    lane = lax.broadcasted_iota(jnp.int32, (64, 256), 1)
    inside = (lane < 128) | ((lane < 192) & (col < 7)) | ((lane >= 192) & (col > 0))

    def one(i, _):
        start = i * 24
        outs = block_rows(wide, [start + b + 8 for b in range(24)], *block_of(0, *weights))
        for b, out in enumerate(outs):
            number = 32 * row - 8 + start + b
            alive = inside & (number >= 0) & (number < 1024)
            middle[start + b] = jnp.where(alive, out, 0.0).astype(BF)
        return _

    lax.fori_loop(0, 2, one, 0)
    rows = [r for b in range(16) for r in (b, b + 16)]
    outs = block_rows(middle, [r + 8 for r in rows], *block_of(1, *weights), narrow=True)
    for r, out in zip(rows, outs):
        second_ref[r] = out.astype(BF)
    for b in range(16):
        pair = jnp.concatenate(outs[2 * b : 2 * b + 2], axis=0).astype(BF)
        turned[pl.ds(b, 128, stride=16), :] = jnp.transpose(pair.astype(F32))
    for m in range(4):
        message_ref[lax.bitwise_xor(members, m)] = turned[512 * m : 512 * m + 512].astype(BF)


def average(place_ref, second_ref, m0, m1, m2, m3, mean_ref, gathered):
    members = place_ref[2]
    for t, ref in enumerate((m0, m1, m2, m3)):
        gathered[lax.bitwise_xor(members, t)] = ref[...]
    for j in range(32):
        blocks = []
        for k in range(4):
            part = gathered[k, 16 * j : 16 * j + 16, :].astype(F32)
            blocks += [part, pltpu.roll(part, 64, 1)]
        mirrored = jnp.transpose(jnp.concatenate(blocks, axis=0))[:64]
        mean_ref[j] = (0.5 * (second_ref[j].astype(F32) + mirrored)).astype(BF)


def last_block(
    spacing_ref, up_ref, own_ref, down_ref, from_left, from_right,
    kernel_ref, gain_ref, shift_ref, expand_ref, out_ref, wide,
):
    weights = (spacing_ref, kernel_ref, gain_ref, shift_ref, expand_ref)
    fill_wide(wide, up_ref, own_ref, down_ref, from_left, from_right)
    outs = block_rows(wide, [r + 8 for r in range(32)], *block_of(2, *weights), narrow=True)
    for r, out in enumerate(outs):
        out_ref[r] = out.astype(BF)


def on_device(contact_map, dilations, conv_weight, conv_gain, conv_shift, out_weight):
    rows, cols = lax.axis_size("row"), lax.axis_size("col")
    row, col = lax.axis_index("row"), lax.axis_index("col")
    mixed = lax.bitwise_xor(lax.rem(row, 4), lax.rem(lax.div(row, 4) + col, 4))
    place = jnp.stack([row, col, mixed]).astype(jnp.int32)
    down_way = [(r, r + 1) for r in range(rows - 1)]
    up_way = [(r + 1, r) for r in range(rows - 1)]
    right_way = [(c, c + 1) for c in range(cols - 1)]
    left_way = [(c + 1, c) for c in range(cols - 1)]

    def rims(own, depth):
        above = lax.ppermute(own[32 - depth :], "row", down_way)
        below = lax.ppermute(own[:depth], "row", up_way)
        strip = jax.ShapeDtypeStruct(((32 + 2 * depth) // 8, 64, 128), BF)
        to_left, to_right = call(
            pack_sides, (strip, strip), (above, own, below), 0, [], 0, 1 << 20
        )
        from_left = lax.ppermute(to_right, "col", right_way)
        from_right = lax.ppermute(to_left, "col", left_way)
        return above, own, below, from_left, from_right

    own = jnp.transpose(contact_map, (1, 0, 2))
    kernel = jnp.transpose(conv_weight.reshape(3, 3, 3, 32, 64), (0, 2, 3, 1, 4)).reshape(3, 96, 192)
    gain = jnp.broadcast_to(conv_gain[:, :, None], (3, 32, 128))
    shift = jnp.broadcast_to(conv_shift[:, :, None], (3, 32, 128))
    weights = (kernel, gain, shift, out_weight)

    tile = jax.ShapeDtypeStruct((32, 64, 128), BF)
    second, messages = call(
        first_blocks,
        (tile, jax.ShapeDtypeStruct((4, 512, 128), BF)),
        (dilations, place, *rims(own, 16), *weights),
        2,
        [
            pltpu.VMEM((64, 64, 256), BF),
            pltpu.VMEM((48, 64, 256), BF),
            pltpu.VMEM((128 * 16, 128), F32),
        ],
        80 * 256 * 64 * 32 * 20,
        4 << 20,
    )
    received = []
    for t in range(4):
        pairs = []
        for a in range(rows // 4):
            for k in range(4):
                for b in range(cols):
                    pairs.append(((4 * a + k) * cols + b, (4 * b + (k ^ t ^ (a + b) % 4)) * cols + a))
        received.append(lax.ppermute(messages[t], BOTH, pairs))
    mean = call(
        average,
        tile,
        (place, second, *received),
        1,
        [pltpu.VMEM((4, 512, 128), BF)],
        0,
        2 << 20,
    )
    out = call(
        last_block,
        tile,
        (dilations, *rims(mean, 8), *weights),
        1,
        [pltpu.VMEM((48, 64, 256), BF)],
        32 * 256 * 64 * 32 * 20,
        2 << 20,
    )
    return jnp.transpose(out, (1, 0, 2))


def solution(mesh):
    return jax.shard_map(
        on_device,
        mesh=mesh,
        in_specs=(P(None, "row", "col"), P(), P(), P(), P(), P()),
        out_specs=P(None, "row", "col"),
        check_vma=False,
    )
```

```python
import functools

import jax
import jax.numpy as jnp
from jax import lax
from jax.experimental import pallas as pl
from jax.experimental.pallas import tpu as pltpu
from jax.sharding import PartitionSpec as P

D = 8
BOTH = ("row", "col")
BF = jnp.bfloat16
F32 = jnp.float32
VMEM = pl.BlockSpec(memory_space=pltpu.VMEM)
SMEM = pl.BlockSpec(memory_space=pltpu.SMEM)
LIMIT = 40 * 1024 * 1024


def call(body, outs, args, n_smem, scratch, flops, moved):
    return pl.pallas_call(
        body,
        out_shape=outs,
        in_specs=[SMEM] * n_smem + [VMEM] * (len(args) - n_smem),
        out_specs=jax.tree.map(lambda _: VMEM, outs),
        scratch_shapes=scratch,
        compiler_params=pltpu.CompilerParams(vmem_limit_bytes=LIMIT),
        cost_estimate=pl.CostEstimate(flops=flops, bytes_accessed=moved, transcendentals=0),
    )(*args)


def lanes(rows):
    return lax.broadcasted_iota(jnp.int32, (rows, 128), 1)


def pack_strips(pieces, start, width):
    lane = lanes(64)
    total = None
    for place, piece in enumerate(pieces):
        moved = pltpu.roll(piece.astype(F32), (place * width - start) % 128, 1)
        total = moved if total is None else jnp.where(lane >= place * width, moved, total)
    return total.astype(BF)


def side_lanes(from_right, from_left, place, width):
    lane = lanes(64)
    right = pltpu.roll(from_right.astype(F32), (-place * width) % 128, 1)
    left = pltpu.roll(from_left.astype(F32), (128 - width - place * width) % 128, 1)
    side = jnp.where(lane < width, right, jnp.where(lane >= 128 - width, left, 0.0))
    return side.astype(BF)


def tap_sums(taps, spacing, narrow):
    lane = lanes(32)
    before, after = lane >= spacing, lane < 128 - spacing
    sums = []
    for tap in taps:
        left = [pltpu.roll(tap[:32, h : h + 128], spacing, 1) for h in (0, 128)]
        right = [pltpu.roll(tap[64:, h : h + 128], 128 - spacing, 1) for h in (0, 128)]
        sums.append(
            [
                tap[32:64, 128 * h : 128 * h + 128]
                + jnp.where(before, left[h], left[1 - h])
                + jnp.where(after, right[h], right[1 - h])
                for h in range(1 if narrow else 2)
            ]
        )
    return sums


def conv_rows(source, rows, spacing, kernel, narrow):
    taps = []
    for at in rows:
        stacked = jnp.concatenate(
            [source[at - spacing], source[at], source[at + spacing]], axis=0
        )
        taps.append(jnp.dot(kernel, jnp.maximum(stacked, 0), preferred_element_type=F32))
    return tap_sums(taps, spacing, narrow)


def grow(sums, gain, shift, expand):
    hidden = [jnp.maximum(gain * conv + shift, 0.0).astype(BF) for conv in sums]
    grown = []
    for i in range(0, len(hidden), 2):
        both = jnp.dot(
            expand, jnp.concatenate(hidden[i : i + 2], axis=1), preferred_element_type=F32
        )
        grown += [both[:, :128], both[:, 128:]]
    return grown


def block_rows(source, rows, spacing, kernel, gain, shift, expand, narrow=False):
    sums = conv_rows(source, rows, spacing, kernel, narrow)
    grown = grow([conv for row in sums for conv in row], gain, shift, expand)
    if narrow:
        return [source[at, :, :128].astype(F32) + g for at, g in zip(rows, grown)]
    return [
        source[at].astype(F32) + jnp.concatenate(grown[2 * i : 2 * i + 2], axis=1)
        for i, at in enumerate(rows)
    ]


def block_of(layer, spacing_ref, kernel_ref, gain_ref, shift_ref, expand_ref):
    return (
        spacing_ref[layer], kernel_ref[layer], gain_ref[layer], shift_ref[layer], expand_ref[layer]
    )


def pack_rows(refs, left_ref, right_ref):
    first = 0
    for ref in refs:
        for g in range(ref.shape[0] // 8):
            pieces = [ref[8 * g + q] for q in range(8)]
            left_ref[first + g] = pack_strips(pieces, 0, 16)
            right_ref[first + g] = pack_strips(pieces, 112, 16)
        first += ref.shape[0] // 8


def pack_sides(up_ref, own_ref, down_ref, left_ref, right_ref):
    pack_rows((up_ref, own_ref, down_ref), left_ref, right_ref)


def fill_wide(wide, refs, from_left, from_right, first=0):
    at = 0
    for ref in refs:
        for r in range(ref.shape[0]):
            wide[first + at, :, :128] = ref[r]
            wide[first + at, :, 128:] = side_lanes(
                from_right[at // 8], from_left[at // 8], at % 8, 16
            )
            at += 1


def first_blocks(
    spacing_ref, place_ref, up_ref, own_ref, down_ref, from_left, from_right,
    kernel_ref, gain_ref, shift_ref, expand_ref,
    second_ref, message_ref, wide, middle, turned,
):
    row, col = place_ref[0], place_ref[1]
    members = place_ref[2]
    weights = (spacing_ref, kernel_ref, gain_ref, shift_ref, expand_ref)
    fill_wide(wide, (up_ref, own_ref, down_ref), from_left, from_right)
    lane = lax.broadcasted_iota(jnp.int32, (64, 256), 1)
    inside = (lane < 128) | ((lane < 192) & (col < 7)) | ((lane >= 192) & (col > 0))

    def one(i, _):
        start = i * 24
        outs = block_rows(wide, [start + b + 8 for b in range(24)], *block_of(0, *weights))
        for b, out in enumerate(outs):
            number = 32 * row - 8 + start + b
            alive = inside & (number >= 0) & (number < 1024)
            middle[start + b] = jnp.where(alive, out, 0.0).astype(BF)
        return _

    lax.fori_loop(0, 2, one, 0)
    rows = [r for b in range(16) for r in (b, b + 16)]
    outs = block_rows(middle, [r + 8 for r in rows], *block_of(1, *weights), narrow=True)
    for r, out in zip(rows, outs):
        second_ref[r] = out.astype(BF)
    for b in range(16):
        pair = jnp.concatenate(outs[2 * b : 2 * b + 2], axis=0).astype(BF)
        turned[pl.ds(b, 128, stride=16), :] = jnp.transpose(pair.astype(F32))
    for m in range(4):
        message_ref[lax.bitwise_xor(members, m)] = turned[512 * m : 512 * m + 512].astype(BF)


def average(place_ref, second_ref, m0, m1, m2, m3, mean_ref, left_ref, right_ref, gathered):
    members = place_ref[2]
    for t, ref in enumerate((m0, m1, m2, m3)):
        gathered[lax.bitwise_xor(members, t)] = ref[...]
    for j in range(32):
        blocks = []
        for k in range(4):
            part = gathered[k, 16 * j : 16 * j + 16, :].astype(F32)
            blocks += [part, pltpu.roll(part, 64, 1)]
        mirrored = jnp.transpose(jnp.concatenate(blocks, axis=0))[:64]
        mean_ref[j] = (0.5 * (second_ref[j].astype(F32) + mirrored)).astype(BF)
    pack_rows((mean_ref,), left_ref, right_ref)


def fill_last(wide, mean_ref, from_left, from_right):
    for at in range(8):
        wide[at] = jnp.zeros((64, 256), BF)
        wide[40 + at] = jnp.zeros((64, 256), BF)
    fill_wide(wide, (mean_ref,), from_left, from_right, 8)


def last_edges(
    spacing_ref, mean_ref, from_left, from_right, kernel_ref, to_up_ref, to_down_ref, wide
):
    spacing, kernel = spacing_ref[2], kernel_ref[2]
    fill_last(wide, mean_ref, from_left, from_right)
    taps = []
    for i in range(8):
        up = jnp.maximum(wide[i + spacing], 0)
        taps.append(jnp.dot(kernel[:, 128:], up, preferred_element_type=F32))
        down = jnp.maximum(wide[40 + i - spacing], 0)
        taps.append(jnp.dot(kernel[:, :64], down, preferred_element_type=F32))
    sums = tap_sums(taps, spacing, True)
    for i in range(8):
        to_up_ref[i] = sums[2 * i][0].astype(BF)
        to_down_ref[i] = sums[2 * i + 1][0].astype(BF)


def last_inner(
    spacing_ref, mean_ref, from_left, from_right, kernel_ref, gain_ref, shift_ref, expand_ref,
    out_ref, conv_ref, wide,
):
    fill_last(wide, mean_ref, from_left, from_right)
    sums = conv_rows(wide, [r + 8 for r in range(32)], spacing_ref[2], kernel_ref[2], True)
    sums = [row[0] for row in sums]
    for i in range(8):
        conv_ref[i] = sums[i]
        conv_ref[8 + i] = sums[24 + i]
    grown = grow(sums[8:24], gain_ref[2], shift_ref[2], expand_ref[2])
    for i in range(16):
        out_ref[8 + i] = (mean_ref[8 + i].astype(F32) + grown[i]).astype(BF)


def last_outer(
    inner_ref, mean_ref, conv_ref, up_ref, down_ref, gain_ref, shift_ref, expand_ref, out_ref
):
    sums = [conv_ref[i] + up_ref[i].astype(F32) for i in range(8)]
    sums += [conv_ref[8 + i] + down_ref[i].astype(F32) for i in range(8)]
    grown = grow(sums, gain_ref[2], shift_ref[2], expand_ref[2])
    out_ref[8:24] = inner_ref[8:24]
    for i in range(16):
        at = i if i < 8 else 16 + i
        out_ref[at] = (mean_ref[at].astype(F32) + grown[i]).astype(BF)


def on_device(contact_map, dilations, conv_weight, conv_gain, conv_shift, out_weight):
    rows, cols = lax.axis_size("row"), lax.axis_size("col")
    row, col = lax.axis_index("row"), lax.axis_index("col")
    mixed = lax.bitwise_xor(lax.rem(row, 4), lax.rem(lax.div(row, 4) + col, 4))
    place = jnp.stack([row, col, mixed]).astype(jnp.int32)
    down_way = [(r, r + 1) for r in range(rows - 1)]
    up_way = [(r + 1, r) for r in range(rows - 1)]
    right_way = [(c, c + 1) for c in range(cols - 1)]
    left_way = [(c + 1, c) for c in range(cols - 1)]

    own = jnp.transpose(contact_map, (1, 0, 2))
    above = lax.ppermute(own[16:], "row", down_way)
    below = lax.ppermute(own[:16], "row", up_way)
    strip = jax.ShapeDtypeStruct((8, 64, 128), BF)
    to_left, to_right = call(
        pack_sides, (strip, strip), (above, own, below), 0, [], 0, 1 << 20
    )
    from_left = lax.ppermute(to_right, "col", right_way)
    from_right = lax.ppermute(to_left, "col", left_way)
    kernel = jnp.transpose(conv_weight.reshape(3, 3, 3, 32, 64), (0, 2, 3, 1, 4)).reshape(3, 96, 192)
    gain = jnp.broadcast_to(conv_gain[:, :, None], (3, 32, 128))
    shift = jnp.broadcast_to(conv_shift[:, :, None], (3, 32, 128))
    weights = (kernel, gain, shift, out_weight)

    tile = jax.ShapeDtypeStruct((32, 64, 128), BF)
    second, messages = call(
        first_blocks,
        (tile, jax.ShapeDtypeStruct((4, 512, 128), BF)),
        (dilations, place, above, own, below, from_left, from_right, *weights),
        2,
        [
            pltpu.VMEM((64, 64, 256), BF),
            pltpu.VMEM((48, 64, 256), BF),
            pltpu.VMEM((128 * 16, 128), F32),
        ],
        80 * 256 * 64 * 32 * 20,
        4 << 20,
    )
    received = []
    for t in range(4):
        pairs = []
        for a in range(rows // 4):
            for k in range(4):
                for b in range(cols):
                    pairs.append(((4 * a + k) * cols + b, (4 * b + (k ^ t ^ (a + b) % 4)) * cols + a))
        received.append(lax.ppermute(messages[t], BOTH, pairs))
    strip = jax.ShapeDtypeStruct((4, 64, 128), BF)
    mean, to_left, to_right = call(
        average,
        (tile, strip, strip),
        (place, second, *received),
        1,
        [pltpu.VMEM((4, 512, 128), BF)],
        0,
        2 << 20,
    )
    from_left = lax.ppermute(to_right, "col", right_way)
    from_right = lax.ppermute(to_left, "col", left_way)
    wide = [pltpu.VMEM((48, 64, 256), BF)]
    edge = jax.ShapeDtypeStruct((8, 32, 128), BF)
    to_up, to_down = call(
        last_edges,
        (edge, edge),
        (dilations, mean, from_left, from_right, kernel),
        1,
        wide,
        16 * 256 * 64 * 96 * 2,
        1 << 20,
    )
    above = lax.ppermute(to_down, "row", down_way)
    below = lax.ppermute(to_up, "row", up_way)
    inner, conv = call(
        last_inner,
        (tile, jax.ShapeDtypeStruct((16, 32, 128), F32)),
        (dilations, mean, from_left, from_right, *weights),
        1,
        wide,
        32 * 256 * 64 * 32 * 20,
        2 << 20,
    )
    out = call(
        last_outer,
        tile,
        (inner, mean, conv, above, below, gain, shift, out_weight),
        0,
        [],
        16 * 256 * 64 * 32 * 2,
        2 << 20,
    )
    return jnp.transpose(out, (1, 0, 2))


def solution(mesh):
    return jax.shard_map(
        on_device,
        mesh=mesh,
        in_specs=(P(None, "row", "col"), P(), P(), P(), P(), P()),
        out_specs=P(None, "row", "col"),
        check_vma=False,
    )
```

```python
import functools

import jax
import jax.numpy as jnp
from jax import lax
from jax.experimental import pallas as pl
from jax.experimental.pallas import tpu as pltpu
from jax.sharding import PartitionSpec as P

D = 8
BOTH = ("row", "col")
BF = jnp.bfloat16
F32 = jnp.float32
VMEM = pl.BlockSpec(memory_space=pltpu.VMEM)
SMEM = pl.BlockSpec(memory_space=pltpu.SMEM)
LIMIT = 40 * 1024 * 1024


def call(body, outs, args, n_smem, scratch, flops, moved):
    return pl.pallas_call(
        body,
        out_shape=outs,
        in_specs=[SMEM] * n_smem + [VMEM] * (len(args) - n_smem),
        out_specs=jax.tree.map(lambda _: VMEM, outs),
        scratch_shapes=scratch,
        compiler_params=pltpu.CompilerParams(vmem_limit_bytes=LIMIT),
        cost_estimate=pl.CostEstimate(flops=flops, bytes_accessed=moved, transcendentals=0),
    )(*args)


def lanes(rows):
    return lax.broadcasted_iota(jnp.int32, (rows, 128), 1)


def pack_strips(pieces, start, width):
    lane = lanes(64)
    total = None
    for place, piece in enumerate(pieces):
        moved = pltpu.roll(piece.astype(F32), (place * width - start) % 128, 1)
        total = moved if total is None else jnp.where(lane >= place * width, moved, total)
    return total.astype(BF)


def side_lanes(from_right, from_left, place, width):
    lane = lanes(64)
    right = pltpu.roll(from_right.astype(F32), (-place * width) % 128, 1)
    left = pltpu.roll(from_left.astype(F32), (128 - width - place * width) % 128, 1)
    side = jnp.where(lane < width, right, jnp.where(lane >= 128 - width, left, 0.0))
    return side.astype(BF)


def tap_sums(taps, spacing, narrow):
    lane = lanes(32)
    before, after = lane >= spacing, lane < 128 - spacing
    sums = []
    for tap in taps:
        left = [pltpu.roll(tap[:32, h : h + 128], spacing, 1) for h in (0, 128)]
        right = [pltpu.roll(tap[64:, h : h + 128], 128 - spacing, 1) for h in (0, 128)]
        sums.append(
            [
                tap[32:64, 128 * h : 128 * h + 128]
                + jnp.where(before, left[h], left[1 - h])
                + jnp.where(after, right[h], right[1 - h])
                for h in range(1 if narrow else 2)
            ]
        )
    return sums


def conv_rows(source, rows, spacing, kernel, narrow):
    taps = []
    for at in rows:
        stacked = jnp.concatenate(
            [source[at - spacing], source[at], source[at + spacing]], axis=0
        )
        taps.append(jnp.dot(kernel, jnp.maximum(stacked, 0), preferred_element_type=F32))
    return tap_sums(taps, spacing, narrow)


def grow(sums, gain, shift, expand):
    hidden = [jnp.maximum(gain * conv + shift, 0.0).astype(BF) for conv in sums]
    grown = []
    for i in range(0, len(hidden), 2):
        both = jnp.dot(
            expand, jnp.concatenate(hidden[i : i + 2], axis=1), preferred_element_type=F32
        )
        grown += [both[:, :128], both[:, 128:]]
    return grown


def block_rows(source, rows, spacing, kernel, gain, shift, expand, narrow=False):
    sums = conv_rows(source, rows, spacing, kernel, narrow)
    grown = grow([conv for row in sums for conv in row], gain, shift, expand)
    if narrow:
        return [source[at, :, :128].astype(F32) + g for at, g in zip(rows, grown)]
    return [
        source[at].astype(F32) + jnp.concatenate(grown[2 * i : 2 * i + 2], axis=1)
        for i, at in enumerate(rows)
    ]


def block_of(layer, spacing_ref, kernel_ref, gain_ref, shift_ref, expand_ref):
    return (
        spacing_ref[layer], kernel_ref[layer], gain_ref[layer], shift_ref[layer], expand_ref[layer]
    )


def pack_rows(refs, place_ref, sides_ref):
    odd = lax.rem(place_ref[1], 2)
    first = 0
    for ref in refs:
        for g in range(ref.shape[0] // 8):
            pieces = [ref[8 * g + q] for q in range(8)]
            sides_ref[1 - odd, first + g] = pack_strips(pieces, 0, 16)
            sides_ref[odd, first + g] = pack_strips(pieces, 112, 16)
        first += ref.shape[0] // 8


def pack_sides(place_ref, up_ref, own_ref, down_ref, sides_ref):
    pack_rows((up_ref, own_ref, down_ref), place_ref, sides_ref)


def fill_wide(wide, refs, place_ref, near_ref, far_ref, first=0):
    odd = lax.rem(place_ref[1], 2) == 1
    at = 0
    for ref in refs:
        for r in range(ref.shape[0]):
            if at % 8 == 0:
                near, far = near_ref[at // 8], far_ref[at // 8]
                from_left, from_right = jnp.where(odd, near, far), jnp.where(odd, far, near)
            wide[first + at, :, :128] = ref[r]
            wide[first + at, :, 128:] = side_lanes(from_right, from_left, at % 8, 16)
            at += 1


def first_blocks(
    spacing_ref, place_ref, up_ref, own_ref, down_ref, near_ref, far_ref,
    kernel_ref, gain_ref, shift_ref, expand_ref,
    second_ref, message_ref, wide, middle, turned,
):
    row, col = place_ref[0], place_ref[1]
    members = place_ref[2]
    weights = (spacing_ref, kernel_ref, gain_ref, shift_ref, expand_ref)
    fill_wide(wide, (up_ref, own_ref, down_ref), place_ref, near_ref, far_ref)
    lane = lax.broadcasted_iota(jnp.int32, (64, 256), 1)
    inside = (lane < 128) | ((lane < 192) & (col < 7)) | ((lane >= 192) & (col > 0))

    def one(i, _):
        start = i * 24
        outs = block_rows(wide, [start + b + 8 for b in range(24)], *block_of(0, *weights))
        for b, out in enumerate(outs):
            number = 32 * row - 8 + start + b
            alive = inside & (number >= 0) & (number < 1024)
            middle[start + b] = jnp.where(alive, out, 0.0).astype(BF)
        return _

    lax.fori_loop(0, 2, one, 0)
    rows = [r for b in range(16) for r in (b, b + 16)]
    outs = block_rows(middle, [r + 8 for r in rows], *block_of(1, *weights), narrow=True)
    for r, out in zip(rows, outs):
        second_ref[r] = out.astype(BF)
    for b in range(16):
        pair = jnp.concatenate(outs[2 * b : 2 * b + 2], axis=0).astype(BF)
        turned[pl.ds(b, 128, stride=16), :] = jnp.transpose(pair.astype(F32))
    for m in range(4):
        message_ref[lax.bitwise_xor(members, m)] = turned[512 * m : 512 * m + 512].astype(BF)


def average(place_ref, second_ref, m0, m1, m2, m3, mean_ref, sides_ref, gathered):
    members = place_ref[2]
    for t, ref in enumerate((m0, m1, m2, m3)):
        gathered[lax.bitwise_xor(members, t)] = ref[...]
    for j in range(32):
        blocks = []
        for k in range(4):
            part = gathered[k, 16 * j : 16 * j + 16, :].astype(F32)
            blocks += [part, pltpu.roll(part, 64, 1)]
        mirrored = jnp.transpose(jnp.concatenate(blocks, axis=0))[:64]
        mean_ref[j] = (0.5 * (second_ref[j].astype(F32) + mirrored)).astype(BF)
    pack_rows((mean_ref,), place_ref, sides_ref)


def fill_last(wide, place_ref, mean_ref, near_ref, far_ref):
    for at in range(8):
        wide[at] = jnp.zeros((64, 256), BF)
        wide[40 + at] = jnp.zeros((64, 256), BF)
    fill_wide(wide, (mean_ref,), place_ref, near_ref, far_ref, 8)


def last_edges(
    spacing_ref, place_ref, mean_ref, near_ref, far_ref, kernel_ref, to_up_ref, to_down_ref, wide
):
    spacing, kernel = spacing_ref[2], kernel_ref[2]
    fill_last(wide, place_ref, mean_ref, near_ref, far_ref)
    taps = []
    for i in range(8):
        up = jnp.maximum(wide[i + spacing], 0)
        taps.append(jnp.dot(kernel[:, 128:], up, preferred_element_type=F32))
        down = jnp.maximum(wide[40 + i - spacing], 0)
        taps.append(jnp.dot(kernel[:, :64], down, preferred_element_type=F32))
    sums = tap_sums(taps, spacing, True)
    for i in range(8):
        to_up_ref[i] = sums[2 * i][0].astype(BF)
        to_down_ref[i] = sums[2 * i + 1][0].astype(BF)


def last_inner(
    spacing_ref, place_ref, mean_ref, near_ref, far_ref, kernel_ref, gain_ref, shift_ref, expand_ref,
    out_ref, conv_ref, wide,
):
    fill_last(wide, place_ref, mean_ref, near_ref, far_ref)
    sums = conv_rows(wide, [r + 8 for r in range(32)], spacing_ref[2], kernel_ref[2], True)
    sums = [row[0] for row in sums]
    for i in range(8):
        conv_ref[i] = sums[i]
        conv_ref[8 + i] = sums[24 + i]
    grown = grow(sums[8:24], gain_ref[2], shift_ref[2], expand_ref[2])
    for i in range(16):
        out_ref[8 + i] = (mean_ref[8 + i].astype(F32) + grown[i]).astype(BF)


def last_outer(
    inner_ref, mean_ref, conv_ref, up_ref, down_ref, gain_ref, shift_ref, expand_ref, out_ref
):
    sums = [conv_ref[i] + up_ref[i].astype(F32) for i in range(8)]
    sums += [conv_ref[8 + i] + down_ref[i].astype(F32) for i in range(8)]
    grown = grow(sums, gain_ref[2], shift_ref[2], expand_ref[2])
    out_ref[8:24] = inner_ref[8:24]
    for i in range(16):
        at = i if i < 8 else 16 + i
        out_ref[at] = (mean_ref[at].astype(F32) + grown[i]).astype(BF)


def on_device(contact_map, dilations, conv_weight, conv_gain, conv_shift, out_weight):
    rows, cols = lax.axis_size("row"), lax.axis_size("col")
    row, col = lax.axis_index("row"), lax.axis_index("col")
    mixed = lax.bitwise_xor(lax.rem(row, 4), lax.rem(lax.div(row, 4) + col, 4))
    place = jnp.stack([row, col, mixed]).astype(jnp.int32)
    down_way = [(r, r + 1) for r in range(rows - 1)]
    up_way = [(r + 1, r) for r in range(rows - 1)]
    near_pairs = [(c, c ^ 1) for c in range(cols)]
    far_pairs = [(c, c + 1) for c in range(1, cols - 1, 2)]
    far_pairs += [(d, c) for c, d in far_pairs]

    own = jnp.transpose(contact_map, (1, 0, 2))
    above = lax.ppermute(own[16:], "row", down_way)
    below = lax.ppermute(own[:16], "row", up_way)
    sides = call(
        pack_sides,
        jax.ShapeDtypeStruct((2, 8, 64, 128), BF),
        (place, above, own, below),
        1,
        [],
        0,
        1 << 20,
    )
    far = lax.ppermute(sides[1], "col", far_pairs)
    near = lax.ppermute(sides[0], "col", near_pairs)
    kernel = jnp.transpose(conv_weight.reshape(3, 3, 3, 32, 64), (0, 2, 3, 1, 4)).reshape(3, 96, 192)
    gain = jnp.broadcast_to(conv_gain[:, :, None], (3, 32, 128))
    shift = jnp.broadcast_to(conv_shift[:, :, None], (3, 32, 128))
    weights = (kernel, gain, shift, out_weight)

    tile = jax.ShapeDtypeStruct((32, 64, 128), BF)
    second, messages = call(
        first_blocks,
        (tile, jax.ShapeDtypeStruct((4, 512, 128), BF)),
        (dilations, place, above, own, below, near, far, *weights),
        2,
        [
            pltpu.VMEM((64, 64, 256), BF),
            pltpu.VMEM((48, 64, 256), BF),
            pltpu.VMEM((128 * 16, 128), F32),
        ],
        80 * 256 * 64 * 32 * 20,
        4 << 20,
    )
    received = []
    for t in range(4):
        pairs = []
        for a in range(rows // 4):
            for k in range(4):
                for b in range(cols):
                    pairs.append(((4 * a + k) * cols + b, (4 * b + (k ^ t ^ (a + b) % 4)) * cols + a))
        received.append(lax.ppermute(messages[t], BOTH, pairs))
    mean, sides = call(
        average,
        (tile, jax.ShapeDtypeStruct((2, 4, 64, 128), BF)),
        (place, second, *received),
        1,
        [pltpu.VMEM((4, 512, 128), BF)],
        0,
        2 << 20,
    )
    far = lax.ppermute(sides[1], "col", far_pairs)
    near = lax.ppermute(sides[0], "col", near_pairs)
    wide = [pltpu.VMEM((48, 64, 256), BF)]
    edge = jax.ShapeDtypeStruct((8, 32, 128), BF)
    to_up, to_down = call(
        last_edges,
        (edge, edge),
        (dilations, place, mean, near, far, kernel),
        2,
        wide,
        16 * 256 * 64 * 96 * 2,
        1 << 20,
    )
    above = lax.ppermute(to_down, "row", down_way)
    below = lax.ppermute(to_up, "row", up_way)
    inner, conv = call(
        last_inner,
        (tile, jax.ShapeDtypeStruct((16, 32, 128), F32)),
        (dilations, place, mean, near, far, *weights),
        2,
        wide,
        32 * 256 * 64 * 32 * 20,
        2 << 20,
    )
    out = call(
        last_outer,
        tile,
        (inner, mean, conv, above, below, gain, shift, out_weight),
        0,
        [],
        16 * 256 * 64 * 32 * 2,
        2 << 20,
    )
    return jnp.transpose(out, (1, 0, 2))


def solution(mesh):
    return jax.shard_map(
        on_device,
        mesh=mesh,
        in_specs=(P(None, "row", "col"), P(), P(), P(), P(), P()),
        out_specs=P(None, "row", "col"),
        check_vma=False,
    )
```

```python
import functools

import jax
import jax.numpy as jnp
from jax import lax
from jax.experimental import pallas as pl
from jax.experimental.pallas import tpu as pltpu
from jax.sharding import PartitionSpec as P

D = 8
BOTH = ("row", "col")
BF = jnp.bfloat16
F32 = jnp.float32
VMEM = pl.BlockSpec(memory_space=pltpu.VMEM)
SMEM = pl.BlockSpec(memory_space=pltpu.SMEM)
LIMIT = 40 * 1024 * 1024


def call(body, outs, args, n_smem, scratch, flops, moved):
    return pl.pallas_call(
        body,
        out_shape=outs,
        in_specs=[SMEM] * n_smem + [VMEM] * (len(args) - n_smem),
        out_specs=jax.tree.map(lambda _: VMEM, outs),
        scratch_shapes=scratch,
        compiler_params=pltpu.CompilerParams(vmem_limit_bytes=LIMIT),
        cost_estimate=pl.CostEstimate(flops=flops, bytes_accessed=moved, transcendentals=0),
    )(*args)


def lanes(rows):
    return lax.broadcasted_iota(jnp.int32, (rows, 128), 1)


def pack_strips(pieces, start, width):
    lane = lanes(64)
    total = None
    for place, piece in enumerate(pieces):
        moved = pltpu.roll(piece.astype(F32), (place * width - start) % 128, 1)
        total = moved if total is None else jnp.where(lane >= place * width, moved, total)
    return total.astype(BF)


def side_lanes(from_right, from_left, place, width):
    lane = lanes(64)
    right = pltpu.roll(from_right.astype(F32), (-place * width) % 128, 1)
    left = pltpu.roll(from_left.astype(F32), (128 - width - place * width) % 128, 1)
    side = jnp.where(lane < width, right, jnp.where(lane >= 128 - width, left, 0.0))
    return side.astype(BF)


def tap_sums(taps, spacing, narrow):
    lane = lanes(32)
    before, after = lane >= spacing, lane < 128 - spacing
    sums = []
    for tap in taps:
        left = [pltpu.roll(tap[:32, h : h + 128], spacing, 1) for h in (0, 128)]
        right = [pltpu.roll(tap[64:, h : h + 128], 128 - spacing, 1) for h in (0, 128)]
        sums.append(
            [
                tap[32:64, 128 * h : 128 * h + 128]
                + jnp.where(before, left[h], left[1 - h])
                + jnp.where(after, right[h], right[1 - h])
                for h in range(1 if narrow else 2)
            ]
        )
    return sums


def conv_rows(source, rows, spacing, kernel, narrow):
    taps = []
    for at in rows:
        stacked = jnp.concatenate(
            [source[at - spacing], source[at], source[at + spacing]], axis=0
        )
        taps.append(jnp.dot(kernel, jnp.maximum(stacked, 0), preferred_element_type=F32))
    return tap_sums(taps, spacing, narrow)


def grow(sums, gain, shift, expand):
    hidden = [jnp.maximum(gain * conv + shift, 0.0).astype(BF) for conv in sums]
    grown = []
    for i in range(0, len(hidden), 2):
        both = jnp.dot(
            expand, jnp.concatenate(hidden[i : i + 2], axis=1), preferred_element_type=F32
        )
        grown += [both[:, :128], both[:, 128:]]
    return grown


def block_rows(source, rows, spacing, kernel, gain, shift, expand, narrow=False):
    sums = conv_rows(source, rows, spacing, kernel, narrow)
    grown = grow([conv for row in sums for conv in row], gain, shift, expand)
    if narrow:
        return [source[at, :, :128].astype(F32) + g for at, g in zip(rows, grown)]
    return [
        source[at].astype(F32) + jnp.concatenate(grown[2 * i : 2 * i + 2], axis=1)
        for i, at in enumerate(rows)
    ]


def block_of(layer, spacing_ref, kernel_ref, gain_ref, shift_ref, expand_ref):
    return (
        spacing_ref[layer], kernel_ref[layer], gain_ref[layer], shift_ref[layer], expand_ref[layer]
    )


def pack_rows(refs, place_ref, sides_ref):
    odd = lax.rem(place_ref[1], 2) == 1
    first = 0
    for ref in refs:
        for g in range(ref.shape[0] // 8):
            pieces = [ref[8 * g + q] for q in range(8)]
            left, right = pack_strips(pieces, 0, 16), pack_strips(pieces, 112, 16)
            sides_ref[0, first + g] = jnp.where(odd, left, right)
            sides_ref[1, first + g] = jnp.where(odd, right, left)
        first += ref.shape[0] // 8


def pack_sides(place_ref, near_row, far_row, own_ref, up_ref, down_ref, sides_ref):
    odd = lax.rem(place_ref[0], 2) == 1
    for r in range(16):
        near, far = near_row[r], far_row[r]
        up_ref[r], down_ref[r] = jnp.where(odd, near, far), jnp.where(odd, far, near)
    pack_rows((up_ref, own_ref, down_ref), place_ref, sides_ref)


def fill_wide(wide, refs, place_ref, near_ref, far_ref, first=0):
    odd = lax.rem(place_ref[1], 2) == 1
    at = 0
    for ref in refs:
        for r in range(ref.shape[0]):
            if at % 8 == 0:
                near, far = near_ref[at // 8], far_ref[at // 8]
                from_left, from_right = jnp.where(odd, near, far), jnp.where(odd, far, near)
            wide[first + at, :, :128] = ref[r]
            wide[first + at, :, 128:] = side_lanes(from_right, from_left, at % 8, 16)
            at += 1


def first_blocks(
    spacing_ref, place_ref, up_ref, own_ref, down_ref, near_ref, far_ref,
    kernel_ref, gain_ref, shift_ref, expand_ref,
    second_ref, message_ref, wide, middle, turned,
):
    row, col = place_ref[0], place_ref[1]
    members = place_ref[2]
    weights = (spacing_ref, kernel_ref, gain_ref, shift_ref, expand_ref)
    fill_wide(wide, (up_ref, own_ref, down_ref), place_ref, near_ref, far_ref)
    lane = lax.broadcasted_iota(jnp.int32, (64, 256), 1)
    inside = (lane < 128) | ((lane < 192) & (col < 7)) | ((lane >= 192) & (col > 0))

    def one(i, _):
        start = i * 24
        outs = block_rows(wide, [start + b + 8 for b in range(24)], *block_of(0, *weights))
        for b, out in enumerate(outs):
            number = 32 * row - 8 + start + b
            alive = inside & (number >= 0) & (number < 1024)
            middle[start + b] = jnp.where(alive, out, 0.0).astype(BF)
        return _

    lax.fori_loop(0, 2, one, 0)
    rows = [r for b in range(16) for r in (b, b + 16)]
    outs = block_rows(middle, [r + 8 for r in rows], *block_of(1, *weights), narrow=True)
    for r, out in zip(rows, outs):
        second_ref[r] = out.astype(BF)
    for b in range(16):
        pair = jnp.concatenate(outs[2 * b : 2 * b + 2], axis=0).astype(BF)
        turned[pl.ds(b, 128, stride=16), :] = jnp.transpose(pair.astype(F32))
    for m in range(4):
        message_ref[lax.bitwise_xor(members, m)] = turned[512 * m : 512 * m + 512].astype(BF)


def average(place_ref, second_ref, m0, m1, m2, m3, mean_ref, sides_ref, gathered):
    members = place_ref[2]
    for t, ref in enumerate((m0, m1, m2, m3)):
        gathered[lax.bitwise_xor(members, t)] = ref[...]
    for j in range(32):
        blocks = []
        for k in range(4):
            part = gathered[k, 16 * j : 16 * j + 16, :].astype(F32)
            blocks += [part, pltpu.roll(part, 64, 1)]
        mirrored = jnp.transpose(jnp.concatenate(blocks, axis=0))[:64]
        mean_ref[j] = (0.5 * (second_ref[j].astype(F32) + mirrored)).astype(BF)
    pack_rows((mean_ref,), place_ref, sides_ref)


def fill_last(wide, place_ref, mean_ref, near_ref, far_ref):
    for at in range(8):
        wide[at] = jnp.zeros((64, 256), BF)
        wide[40 + at] = jnp.zeros((64, 256), BF)
    fill_wide(wide, (mean_ref,), place_ref, near_ref, far_ref, 8)


def last_edges(
    spacing_ref, place_ref, mean_ref, near_ref, far_ref, kernel_ref, near_row, far_row, wide
):
    spacing, kernel = spacing_ref[2], kernel_ref[2]
    odd = lax.rem(place_ref[0], 2) == 1
    fill_last(wide, place_ref, mean_ref, near_ref, far_ref)
    taps = []
    for i in range(8):
        up = jnp.maximum(wide[i + spacing], 0)
        taps.append(jnp.dot(kernel[:, 128:], up, preferred_element_type=F32))
        down = jnp.maximum(wide[40 + i - spacing], 0)
        taps.append(jnp.dot(kernel[:, :64], down, preferred_element_type=F32))
    sums = tap_sums(taps, spacing, True)
    for i in range(8):
        up, down = sums[2 * i][0], sums[2 * i + 1][0]
        near_row[i] = jnp.where(odd, up, down).astype(BF)
        far_row[i] = jnp.where(odd, down, up).astype(BF)


def last_inner(
    spacing_ref, place_ref, mean_ref, near_ref, far_ref, kernel_ref, gain_ref, shift_ref, expand_ref,
    out_ref, conv_ref, wide,
):
    fill_last(wide, place_ref, mean_ref, near_ref, far_ref)
    sums = conv_rows(wide, [r + 8 for r in range(32)], spacing_ref[2], kernel_ref[2], True)
    sums = [row[0] for row in sums]
    for i in range(8):
        conv_ref[i] = sums[i]
        conv_ref[8 + i] = sums[24 + i]
    grown = grow(sums[8:24], gain_ref[2], shift_ref[2], expand_ref[2])
    for i in range(16):
        out_ref[8 + i] = (mean_ref[8 + i].astype(F32) + grown[i]).astype(BF)


def last_outer(
    place_ref, inner_ref, mean_ref, conv_ref, near_row, far_row, gain_ref, shift_ref, expand_ref,
    out_ref,
):
    odd = lax.rem(place_ref[0], 2) == 1
    near = [near_row[i].astype(F32) for i in range(8)]
    far = [far_row[i].astype(F32) for i in range(8)]
    sums = [conv_ref[i] + jnp.where(odd, near[i], far[i]) for i in range(8)]
    sums += [conv_ref[8 + i] + jnp.where(odd, far[i], near[i]) for i in range(8)]
    grown = grow(sums, gain_ref[2], shift_ref[2], expand_ref[2])
    out_ref[8:24] = inner_ref[8:24]
    for i in range(16):
        at = i if i < 8 else 16 + i
        out_ref[at] = (mean_ref[at].astype(F32) + grown[i]).astype(BF)


def on_device(contact_map, dilations, conv_weight, conv_gain, conv_shift, out_weight):
    rows, cols = lax.axis_size("row"), lax.axis_size("col")
    row, col = lax.axis_index("row"), lax.axis_index("col")
    mixed = lax.bitwise_xor(lax.rem(row, 4), lax.rem(lax.div(row, 4) + col, 4))
    place = jnp.stack([row, col, mixed]).astype(jnp.int32)
    near_rows = [(r, r ^ 1) for r in range(rows)]
    far_rows = [(r, r + 1) for r in range(1, rows - 1, 2)]
    far_rows += [(d, r) for r, d in far_rows]
    near_pairs = [(c, c ^ 1) for c in range(cols)]
    far_pairs = [(c, c + 1) for c in range(1, cols - 1, 2)]
    far_pairs += [(d, c) for c, d in far_pairs]

    own = jnp.transpose(contact_map, (1, 0, 2))
    odd_row = lax.rem(row, 2)
    far_row = lax.ppermute(
        lax.dynamic_slice_in_dim(own, 16 * odd_row, 16, 0), "row", far_rows
    )
    near_row = lax.ppermute(
        lax.dynamic_slice_in_dim(own, 16 - 16 * odd_row, 16, 0), "row", near_rows
    )
    rim = jax.ShapeDtypeStruct((16, 64, 128), BF)
    above, below, sides = call(
        pack_sides,
        (rim, rim, jax.ShapeDtypeStruct((2, 8, 64, 128), BF)),
        (place, near_row, far_row, own),
        1,
        [],
        0,
        1 << 20,
    )
    far = lax.ppermute(sides[1], "col", far_pairs)
    near = lax.ppermute(sides[0], "col", near_pairs)
    kernel = jnp.transpose(conv_weight.reshape(3, 3, 3, 32, 64), (0, 2, 3, 1, 4)).reshape(3, 96, 192)
    gain = jnp.broadcast_to(conv_gain[:, :, None], (3, 32, 128))
    shift = jnp.broadcast_to(conv_shift[:, :, None], (3, 32, 128))
    weights = (kernel, gain, shift, out_weight)

    tile = jax.ShapeDtypeStruct((32, 64, 128), BF)
    second, messages = call(
        first_blocks,
        (tile, jax.ShapeDtypeStruct((4, 512, 128), BF)),
        (dilations, place, above, own, below, near, far, *weights),
        2,
        [
            pltpu.VMEM((64, 64, 256), BF),
            pltpu.VMEM((48, 64, 256), BF),
            pltpu.VMEM((128 * 16, 128), F32),
        ],
        80 * 256 * 64 * 32 * 20,
        4 << 20,
    )
    received = []
    for t in range(4):
        pairs = []
        for a in range(rows // 4):
            for k in range(4):
                for b in range(cols):
                    pairs.append(((4 * a + k) * cols + b, (4 * b + (k ^ t ^ (a + b) % 4)) * cols + a))
        received.append(lax.ppermute(messages[t], BOTH, pairs))
    mean, sides = call(
        average,
        (tile, jax.ShapeDtypeStruct((2, 4, 64, 128), BF)),
        (place, second, *received),
        1,
        [pltpu.VMEM((4, 512, 128), BF)],
        0,
        2 << 20,
    )
    far = lax.ppermute(sides[1], "col", far_pairs)
    near = lax.ppermute(sides[0], "col", near_pairs)
    wide = [pltpu.VMEM((48, 64, 256), BF)]
    edge = jax.ShapeDtypeStruct((8, 32, 128), BF)
    to_near, to_far = call(
        last_edges,
        (edge, edge),
        (dilations, place, mean, near, far, kernel),
        2,
        wide,
        16 * 256 * 64 * 96 * 2,
        1 << 20,
    )
    far_row = lax.ppermute(to_far, "row", far_rows)
    near_row = lax.ppermute(to_near, "row", near_rows)
    inner, conv = call(
        last_inner,
        (tile, jax.ShapeDtypeStruct((16, 32, 128), F32)),
        (dilations, place, mean, near, far, *weights),
        2,
        wide,
        32 * 256 * 64 * 32 * 20,
        2 << 20,
    )
    out = call(
        last_outer,
        tile,
        (place, inner, mean, conv, near_row, far_row, gain, shift, out_weight),
        1,
        [],
        16 * 256 * 64 * 32 * 2,
        2 << 20,
    )
    return jnp.transpose(out, (1, 0, 2))


def solution(mesh):
    return jax.shard_map(
        on_device,
        mesh=mesh,
        in_specs=(P(None, "row", "col"), P(), P(), P(), P(), P()),
        out_specs=P(None, "row", "col"),
        check_vma=False,
    )
```

```python
import functools

import jax
import jax.numpy as jnp
from jax import lax
from jax.experimental import pallas as pl
from jax.experimental.pallas import tpu as pltpu
from jax.sharding import PartitionSpec as P

D = 8
BOTH = ("row", "col")
BF = jnp.bfloat16
F32 = jnp.float32
VMEM = pl.BlockSpec(memory_space=pltpu.VMEM)
SMEM = pl.BlockSpec(memory_space=pltpu.SMEM)
LIMIT = 40 * 1024 * 1024


def call(body, outs, args, n_smem, scratch, flops, moved):
    return pl.pallas_call(
        body,
        out_shape=outs,
        in_specs=[SMEM] * n_smem + [VMEM] * (len(args) - n_smem),
        out_specs=jax.tree.map(lambda _: VMEM, outs),
        scratch_shapes=scratch,
        compiler_params=pltpu.CompilerParams(vmem_limit_bytes=LIMIT),
        cost_estimate=pl.CostEstimate(flops=flops, bytes_accessed=moved, transcendentals=0),
    )(*args)


def lanes(rows):
    return lax.broadcasted_iota(jnp.int32, (rows, 128), 1)


def pack_strips(pieces, start, width):
    lane = lanes(64)
    total = None
    for place, piece in enumerate(pieces):
        moved = pltpu.roll(piece.astype(F32), (place * width - start) % 128, 1)
        total = moved if total is None else jnp.where(lane >= place * width, moved, total)
    return total


def side_lanes(from_right, from_left, place, width):
    lane = lanes(64)
    right = pltpu.roll(from_right.astype(F32), (-place * width) % 128, 1)
    left = pltpu.roll(from_left.astype(F32), (128 - width - place * width) % 128, 1)
    side = jnp.where(lane < width, right, jnp.where(lane >= 128 - width, left, 0.0))
    return side.astype(BF)


def tap_sums(taps, spacing, narrow):
    lane = lanes(32)
    before, after = lane >= spacing, lane < 128 - spacing
    sums = []
    for tap in taps:
        left = [pltpu.roll(tap[:32, h : h + 128], spacing, 1) for h in (0, 128)]
        right = [pltpu.roll(tap[64:, h : h + 128], 128 - spacing, 1) for h in (0, 128)]
        sums.append(
            [
                tap[32:64, 128 * h : 128 * h + 128]
                + jnp.where(before, left[h], left[1 - h])
                + jnp.where(after, right[h], right[1 - h])
                for h in range(1 if narrow else 2)
            ]
        )
    return sums


def conv_rows(source, rows, spacing, kernel, narrow):
    taps = []
    for at in rows:
        stacked = jnp.concatenate(
            [source[at - spacing], source[at], source[at + spacing]], axis=0
        )
        taps.append(jnp.dot(kernel, jnp.maximum(stacked, 0), preferred_element_type=F32))
    return tap_sums(taps, spacing, narrow)


def grow(sums, gain, shift, expand):
    hidden = [jnp.maximum(gain * conv + shift, 0.0).astype(BF) for conv in sums]
    grown = []
    for i in range(0, len(hidden), 2):
        both = jnp.dot(
            expand, jnp.concatenate(hidden[i : i + 2], axis=1), preferred_element_type=F32
        )
        grown += [both[:, :128], both[:, 128:]]
    return grown


def block_rows(source, rows, spacing, kernel, gain, shift, expand, narrow=False):
    sums = conv_rows(source, rows, spacing, kernel, narrow)
    grown = grow([conv for row in sums for conv in row], gain, shift, expand)
    if narrow:
        return [source[at, :, :128].astype(F32) + g for at, g in zip(rows, grown)]
    return [
        source[at].astype(F32) + jnp.concatenate(grown[2 * i : 2 * i + 2], axis=1)
        for i, at in enumerate(rows)
    ]


def block_of(layer, spacing_ref, kernel_ref, gain_ref, shift_ref, expand_ref):
    return (
        spacing_ref[layer], kernel_ref[layer], gain_ref[layer], shift_ref[layer], expand_ref[layer]
    )


def pack_rows(rows, place_ref, sides_ref):
    odd = lax.rem(place_ref[1], 2) == 1
    for g in range(len(rows) // 8):
        pieces = rows[8 * g : 8 * g + 8]
        left, right = pack_strips(pieces, 0, 16), pack_strips(pieces, 112, 16)
        sides_ref[0, g] = jnp.where(odd, left, right).astype(BF)
        sides_ref[1, g] = jnp.where(odd, right, left).astype(BF)


def pack_sides(place_ref, near_row, far_row, own_ref, up_ref, down_ref, sides_ref):
    odd = lax.rem(place_ref[0], 2) == 1
    up, down = [], []
    for r in range(16):
        near, far = near_row[r], far_row[r]
        up.append(jnp.where(odd, near, far))
        down.append(jnp.where(odd, far, near))
        up_ref[r], down_ref[r] = up[r], down[r]
    pack_rows(up + [own_ref[r] for r in range(32)] + down, place_ref, sides_ref)


def fill_wide(wide, refs, place_ref, near_ref, far_ref, first=0):
    odd = lax.rem(place_ref[1], 2) == 1
    at = 0
    for ref in refs:
        for r in range(ref.shape[0]):
            if at % 8 == 0:
                near, far = near_ref[at // 8], far_ref[at // 8]
                from_left, from_right = jnp.where(odd, near, far), jnp.where(odd, far, near)
            wide[first + at, :, :128] = ref[r]
            wide[first + at, :, 128:] = side_lanes(from_right, from_left, at % 8, 16)
            at += 1


def first_blocks(
    spacing_ref, place_ref, up_ref, own_ref, down_ref, near_ref, far_ref,
    kernel_ref, gain_ref, shift_ref, expand_ref,
    second_ref, message_ref, wide, middle, turned,
):
    row, col = place_ref[0], place_ref[1]
    members = place_ref[2]
    weights = (spacing_ref, kernel_ref, gain_ref, shift_ref, expand_ref)
    fill_wide(wide, (up_ref, own_ref, down_ref), place_ref, near_ref, far_ref)
    lane = lax.broadcasted_iota(jnp.int32, (64, 256), 1)
    inside = (lane < 128) | ((lane < 192) & (col < 7)) | ((lane >= 192) & (col > 0))

    def one(i, _):
        start = i * 24
        outs = block_rows(wide, [start + b + 8 for b in range(24)], *block_of(0, *weights))
        for b, out in enumerate(outs):
            number = 32 * row - 8 + start + b
            alive = inside & (number >= 0) & (number < 1024)
            middle[start + b] = jnp.where(alive, out, 0.0).astype(BF)
        return _

    lax.fori_loop(0, 2, one, 0)
    rows = [r for b in range(16) for r in (b, b + 16)]
    outs = block_rows(middle, [r + 8 for r in rows], *block_of(1, *weights), narrow=True)
    for r, out in zip(rows, outs):
        second_ref[r] = out.astype(BF)
    for b in range(16):
        pair = jnp.concatenate(outs[2 * b : 2 * b + 2], axis=0).astype(BF)
        turned[pl.ds(b, 128, stride=16), :] = jnp.transpose(pair.astype(F32))
    for m in range(4):
        message_ref[lax.bitwise_xor(members, m)] = turned[512 * m : 512 * m + 512].astype(BF)


def average(place_ref, second_ref, m0, m1, m2, m3, mean_ref, sides_ref, gathered):
    members = place_ref[2]
    for t, ref in enumerate((m0, m1, m2, m3)):
        gathered[lax.bitwise_xor(members, t)] = ref[...]
    mean = []
    for j in range(32):
        blocks = []
        for k in range(4):
            part = gathered[k, 16 * j : 16 * j + 16, :].astype(F32)
            blocks += [part, pltpu.roll(part, 64, 1)]
        mirrored = jnp.transpose(jnp.concatenate(blocks, axis=0))[:64]
        mean.append((0.5 * (second_ref[j].astype(F32) + mirrored)).astype(BF))
        mean_ref[j] = mean[j]
    pack_rows(mean, place_ref, sides_ref)


def fill_last(wide, place_ref, mean_ref, near_ref, far_ref):
    for at in range(8):
        wide[at] = jnp.zeros((64, 256), BF)
        wide[40 + at] = jnp.zeros((64, 256), BF)
    fill_wide(wide, (mean_ref,), place_ref, near_ref, far_ref, 8)


def last_edges(
    spacing_ref, place_ref, mean_ref, near_ref, far_ref, kernel_ref, near_row, far_row, wide
):
    spacing, kernel = spacing_ref[2], kernel_ref[2]
    odd = lax.rem(place_ref[0], 2) == 1
    fill_last(wide, place_ref, mean_ref, near_ref, far_ref)
    taps = []
    for i in range(8):
        up = jnp.maximum(wide[i + spacing], 0)
        taps.append(jnp.dot(kernel[:, 128:], up, preferred_element_type=F32))
        down = jnp.maximum(wide[40 + i - spacing], 0)
        taps.append(jnp.dot(kernel[:, :64], down, preferred_element_type=F32))
    sums = tap_sums(taps, spacing, True)
    for i in range(8):
        up, down = sums[2 * i][0], sums[2 * i + 1][0]
        near_row[i] = jnp.where(odd, up, down).astype(BF)
        far_row[i] = jnp.where(odd, down, up).astype(BF)


def last_inner(
    spacing_ref, place_ref, mean_ref, near_ref, far_ref, kernel_ref, gain_ref, shift_ref, expand_ref,
    out_ref, conv_ref, wide,
):
    fill_last(wide, place_ref, mean_ref, near_ref, far_ref)
    sums = conv_rows(wide, [r + 8 for r in range(32)], spacing_ref[2], kernel_ref[2], True)
    sums = [row[0] for row in sums]
    for i in range(8):
        conv_ref[i] = sums[i]
        conv_ref[8 + i] = sums[24 + i]
    grown = grow(sums[8:24], gain_ref[2], shift_ref[2], expand_ref[2])
    for i in range(16):
        out_ref[8 + i] = (mean_ref[8 + i].astype(F32) + grown[i]).astype(BF)


def last_outer(
    place_ref, inner_ref, mean_ref, conv_ref, near_row, far_row, gain_ref, shift_ref, expand_ref,
    out_ref,
):
    odd = lax.rem(place_ref[0], 2) == 1
    near = [near_row[i].astype(F32) for i in range(8)]
    far = [far_row[i].astype(F32) for i in range(8)]
    sums = [conv_ref[i] + jnp.where(odd, near[i], far[i]) for i in range(8)]
    sums += [conv_ref[8 + i] + jnp.where(odd, far[i], near[i]) for i in range(8)]
    grown = grow(sums, gain_ref[2], shift_ref[2], expand_ref[2])
    out_ref[8:24] = inner_ref[8:24]
    for i in range(16):
        at = i if i < 8 else 16 + i
        out_ref[at] = (mean_ref[at].astype(F32) + grown[i]).astype(BF)


def on_device(contact_map, dilations, conv_weight, conv_gain, conv_shift, out_weight):
    rows, cols = lax.axis_size("row"), lax.axis_size("col")
    row, col = lax.axis_index("row"), lax.axis_index("col")
    mixed = lax.bitwise_xor(lax.rem(row, 4), lax.rem(lax.div(row, 4) + col, 4))
    place = jnp.stack([row, col, mixed]).astype(jnp.int32)
    near_rows = [(r, r ^ 1) for r in range(rows)]
    far_rows = [(r, r + 1) for r in range(1, rows - 1, 2)]
    far_rows += [(d, r) for r, d in far_rows]
    near_pairs = [(c, c ^ 1) for c in range(cols)]
    far_pairs = [(c, c + 1) for c in range(1, cols - 1, 2)]
    far_pairs += [(d, c) for c, d in far_pairs]

    own = jnp.transpose(contact_map, (1, 0, 2))
    odd_row = lax.rem(row, 2)

    def row_rims(depth):
        def exchange(own, odd):
            first, last = (32 - depth) * odd, (32 - depth) * (1 - odd)
            far = lax.ppermute(lax.dynamic_slice_in_dim(own, first, depth, 0), "row", far_rows)
            near = lax.ppermute(lax.dynamic_slice_in_dim(own, last, depth, 0), "row", near_rows)
            empty = jnp.zeros((16, 64, 128), BF)
            spare = 16 - depth
            return (
                lax.dynamic_update_slice_in_dim(empty, far, spare * (1 - odd), 0),
                lax.dynamic_update_slice_in_dim(empty, near, spare * odd, 0),
            )

        return exchange

    reach = dilations[0] + dilations[1]
    far_row, near_row = lax.switch(
        lax.div(reach - 1, 2), [row_rims(depth) for depth in range(2, 17, 2)], own, odd_row
    )
    rim = jax.ShapeDtypeStruct((16, 64, 128), BF)
    above, below, sides = call(
        pack_sides,
        (rim, rim, jax.ShapeDtypeStruct((2, 8, 64, 128), BF)),
        (place, near_row, far_row, own),
        1,
        [],
        0,
        1 << 20,
    )
    far = lax.ppermute(sides[1], "col", far_pairs)
    near = lax.ppermute(sides[0], "col", near_pairs)
    kernel = jnp.transpose(conv_weight.reshape(3, 3, 3, 32, 64), (0, 2, 3, 1, 4)).reshape(3, 96, 192)
    gain = jnp.broadcast_to(conv_gain[:, :, None], (3, 32, 128))
    shift = jnp.broadcast_to(conv_shift[:, :, None], (3, 32, 128))
    weights = (kernel, gain, shift, out_weight)

    tile = jax.ShapeDtypeStruct((32, 64, 128), BF)
    second, messages = call(
        first_blocks,
        (tile, jax.ShapeDtypeStruct((4, 512, 128), BF)),
        (dilations, place, above, own, below, near, far, *weights),
        2,
        [
            pltpu.VMEM((64, 64, 256), BF),
            pltpu.VMEM((48, 64, 256), BF),
            pltpu.VMEM((128 * 16, 128), F32),
        ],
        80 * 256 * 64 * 32 * 20,
        4 << 20,
    )
    received = []
    for t in range(4):
        pairs = []
        for a in range(rows // 4):
            for k in range(4):
                for b in range(cols):
                    pairs.append(((4 * a + k) * cols + b, (4 * b + (k ^ t ^ (a + b) % 4)) * cols + a))
        received.append(lax.ppermute(messages[t], BOTH, pairs))
    mean, sides = call(
        average,
        (tile, jax.ShapeDtypeStruct((2, 4, 64, 128), BF)),
        (place, second, *received),
        1,
        [pltpu.VMEM((4, 512, 128), BF)],
        0,
        2 << 20,
    )
    far = lax.ppermute(sides[1], "col", far_pairs)
    near = lax.ppermute(sides[0], "col", near_pairs)
    wide = [pltpu.VMEM((48, 64, 256), BF)]
    edge = jax.ShapeDtypeStruct((8, 32, 128), BF)
    to_near, to_far = call(
        last_edges,
        (edge, edge),
        (dilations, place, mean, near, far, kernel),
        2,
        wide,
        16 * 256 * 64 * 96 * 2,
        1 << 20,
    )
    far_row = lax.ppermute(to_far, "row", far_rows)
    near_row = lax.ppermute(to_near, "row", near_rows)
    inner, conv = call(
        last_inner,
        (tile, jax.ShapeDtypeStruct((16, 32, 128), F32)),
        (dilations, place, mean, near, far, *weights),
        2,
        wide,
        32 * 256 * 64 * 32 * 20,
        2 << 20,
    )
    out = call(
        last_outer,
        tile,
        (place, inner, mean, conv, near_row, far_row, gain, shift, out_weight),
        1,
        [],
        16 * 256 * 64 * 32 * 2,
        2 << 20,
    )
    return jnp.transpose(out, (1, 0, 2))


def solution(mesh):
    return jax.shard_map(
        on_device,
        mesh=mesh,
        in_specs=(P(None, "row", "col"), P(), P(), P(), P(), P()),
        out_specs=P(None, "row", "col"),
        check_vma=False,
    )
```

```python
import functools

import jax
import jax.numpy as jnp
from jax import lax
from jax.experimental import pallas as pl
from jax.experimental.pallas import tpu as pltpu
from jax.sharding import PartitionSpec as P

D = 8
BOTH = ("row", "col")
BF = jnp.bfloat16
F32 = jnp.float32
VMEM = pl.BlockSpec(memory_space=pltpu.VMEM)
SMEM = pl.BlockSpec(memory_space=pltpu.SMEM)
LIMIT = 40 * 1024 * 1024


def call(body, outs, args, n_smem, scratch, flops, moved):
    return pl.pallas_call(
        body,
        out_shape=outs,
        in_specs=[SMEM] * n_smem + [VMEM] * (len(args) - n_smem),
        out_specs=jax.tree.map(lambda _: VMEM, outs),
        scratch_shapes=scratch,
        compiler_params=pltpu.CompilerParams(vmem_limit_bytes=LIMIT),
        cost_estimate=pl.CostEstimate(flops=flops, bytes_accessed=moved, transcendentals=0),
    )(*args)


def lanes(rows):
    return lax.broadcasted_iota(jnp.int32, (rows, 128), 1)


def pack_strips(pieces, start, width):
    lane = lanes(64)
    total = None
    for place, piece in enumerate(pieces):
        moved = pltpu.roll(piece.astype(F32), (place * width - start) % 128, 1)
        total = moved if total is None else jnp.where(lane >= place * width, moved, total)
    return total


def side_lanes(from_right, from_left, place, width):
    lane = lanes(64)
    right = pltpu.roll(from_right.astype(F32), (-place * width) % 128, 1)
    left = pltpu.roll(from_left.astype(F32), (128 - width - place * width) % 128, 1)
    side = jnp.where(lane < width, right, jnp.where(lane >= 128 - width, left, 0.0))
    return side.astype(BF)


def tap_sums(taps, spacing, narrow):
    lane = lanes(32)
    before, after = lane >= spacing, lane < 128 - spacing
    sums = []
    for tap in taps:
        left = [pltpu.roll(tap[:32, h : h + 128], spacing, 1) for h in (0, 128)]
        right = [pltpu.roll(tap[64:, h : h + 128], 128 - spacing, 1) for h in (0, 128)]
        sums.append(
            [
                tap[32:64, 128 * h : 128 * h + 128]
                + jnp.where(before, left[h], left[1 - h])
                + jnp.where(after, right[h], right[1 - h])
                for h in range(1 if narrow else 2)
            ]
        )
    return sums


def conv_rows(source, rows, spacing, kernel, narrow):
    taps = []
    for at in rows:
        stacked = jnp.concatenate(
            [source[at - spacing], source[at], source[at + spacing]], axis=0
        )
        taps.append(jnp.dot(kernel, jnp.maximum(stacked, 0), preferred_element_type=F32))
    return tap_sums(taps, spacing, narrow)


def grow(sums, gain, shift, expand):
    hidden = [jnp.maximum(gain * conv + shift, 0.0).astype(BF) for conv in sums]
    grown = []
    for i in range(0, len(hidden), 2):
        both = jnp.dot(
            expand, jnp.concatenate(hidden[i : i + 2], axis=1), preferred_element_type=F32
        )
        grown += [both[:, :128], both[:, 128:]]
    return grown


def block_rows(source, rows, spacing, kernel, gain, shift, expand, narrow=False):
    sums = conv_rows(source, rows, spacing, kernel, narrow)
    grown = grow([conv for row in sums for conv in row], gain, shift, expand)
    if narrow:
        return [source[at, :, :128].astype(F32) + g for at, g in zip(rows, grown)]
    return [
        source[at].astype(F32) + jnp.concatenate(grown[2 * i : 2 * i + 2], axis=1)
        for i, at in enumerate(rows)
    ]


def block_of(layer, spacing_ref, kernel_ref, gain_ref, shift_ref, expand_ref):
    return (
        spacing_ref[layer], kernel_ref[layer], gain_ref[layer], shift_ref[layer], expand_ref[layer]
    )


def pack_rows(rows, odd, sides_ref):
    for g in range(len(rows) // 8):
        pieces = rows[8 * g : 8 * g + 8]
        left, right = pack_strips(pieces, 0, 16), pack_strips(pieces, 112, 16)
        sides_ref[0, g] = jnp.where(odd, left, right).astype(BF)
        sides_ref[1, g] = jnp.where(odd, right, left).astype(BF)


def pack_sides(parity_ref, near_row, far_row, own_ref, sides_ref):
    odd = jnp.broadcast_to(parity_ref[1], (64, 128)) == 1
    rows = [ref[r] for ref in (near_row, own_ref, far_row) for r in range(ref.shape[0])]
    pack_rows(rows, odd, sides_ref)


def fill_wide(wide, parts, odd_col, near_ref, far_ref):
    for ref, count, source, start, block in parts:
        for r in range(count):
            if r % 8 == 0:
                near, far = near_ref[block + r // 8], far_ref[block + r // 8]
                from_left = jnp.where(odd_col, near, far)
                from_right = jnp.where(odd_col, far, near)
            wide[start + r, :, :128] = ref[source + r]
            wide[start + r, :, 128:] = side_lanes(from_right, from_left, r % 8, 16)


def first_blocks(
    scalar_ref, near_row, own_ref, far_row, near_ref, far_ref,
    kernel_ref, gain_ref, shift_ref, expand_ref,
    second_ref, message_ref, wide, middle, turned,
):
    row, col, members = scalar_ref[3], scalar_ref[4], scalar_ref[5]
    weights = (scalar_ref, kernel_ref, gain_ref, shift_ref, expand_ref)
    far_start = 48 * lax.rem(row, 2)
    parts = (
        (near_row, 16, 0, 48 - far_start, 0),
        (own_ref, 32, 0, 16, 2),
        (far_row, 16, 0, far_start, 6),
    )
    fill_wide(wide, parts, lax.rem(col, 2) == 1, near_ref, far_ref)
    lane = lax.broadcasted_iota(jnp.int32, (64, 256), 1)
    inside = (lane < 128) | ((lane < 192) & (col < 7)) | ((lane >= 192) & (col > 0))

    outs = block_rows(wide, [r + 8 for r in range(48)], *block_of(0, *weights))
    for r, out in enumerate(outs):
        alive = inside
        if not 8 <= r < 40:
            number = 32 * row - 8 + r
            alive = inside & (number >= 0) & (number < 1024)
        middle[r] = jnp.where(alive, out, 0.0).astype(BF)
    rows = [r for b in range(16) for r in (b, b + 16)]
    outs = block_rows(middle, [r + 8 for r in rows], *block_of(1, *weights), narrow=True)
    for r, out in zip(rows, outs):
        second_ref[r] = out.astype(BF)
    for b in range(16):
        pair = jnp.concatenate(outs[2 * b : 2 * b + 2], axis=0).astype(BF)
        turned[pl.ds(b, 128, stride=16), :] = jnp.transpose(pair.astype(F32))
    for m in range(4):
        message_ref[lax.bitwise_xor(members, m)] = turned[512 * m : 512 * m + 512].astype(BF)


def average(scalar_ref, second_ref, m0, m1, m2, m3, mean_ref, sides_ref, gathered):
    members = scalar_ref[5]
    for t, ref in enumerate((m0, m1, m2, m3)):
        gathered[lax.bitwise_xor(members, t)] = ref[...]
    mean = []
    for j in range(32):
        blocks = []
        for k in range(4):
            part = gathered[k, 16 * j : 16 * j + 16, :].astype(F32)
            blocks += [part, pltpu.roll(part, 64, 1)]
        mirrored = jnp.transpose(jnp.concatenate(blocks, axis=0))[:64]
        mean.append((0.5 * (second_ref[j].astype(F32) + mirrored)).astype(BF))
        mean_ref[j] = mean[j]
    pack_rows(mean, lax.rem(scalar_ref[4], 2) == 1, sides_ref)


def last_edge(to_near, scalar_ref, mean_ref, near_ref, far_ref, kernel_ref, *rest):
    edge_ref, wide = rest[-2:]
    spacing = scalar_ref[2]
    odd = lax.rem(scalar_ref[3], 2)
    up = odd if to_near else 1 - odd
    down = 1 - up
    for r in range(8):
        wide[8 * down + r] = jnp.zeros((64, 256), BF)
    parts = ((mean_ref, 8, 24 * down, 8 * up, 3 * down),)
    fill_wide(wide, parts, lax.rem(scalar_ref[4], 2) == 1, near_ref, far_ref)
    kernel = kernel_ref[2]
    kernel = jnp.where(up == 1, kernel[:, 128:], kernel[:, :64])
    start = jnp.where(up == 1, spacing, 8 - spacing)
    taps = [
        jnp.dot(kernel, jnp.maximum(wide[start + i], 0), preferred_element_type=F32)
        for i in range(8)
    ]
    for i, conv in enumerate(tap_sums(taps, spacing, True)):
        edge_ref[i] = conv[0].astype(BF)


def last_inner(
    scalar_ref, mean_ref, near_ref, far_ref, kernel_ref, gain_ref, shift_ref, expand_ref,
    out_ref, conv_ref, wide,
):
    for at in range(8):
        wide[at] = jnp.zeros((64, 256), BF)
        wide[40 + at] = jnp.zeros((64, 256), BF)
    parts = ((mean_ref, 32, 0, 8, 0),)
    fill_wide(wide, parts, lax.rem(scalar_ref[4], 2) == 1, near_ref, far_ref)
    sums = conv_rows(wide, [r + 8 for r in range(32)], scalar_ref[2], kernel_ref[2], True)
    sums = [row[0] for row in sums]
    for i in range(8):
        conv_ref[i] = sums[i]
        conv_ref[8 + i] = sums[24 + i]
    grown = grow(sums[8:24], gain_ref[2], shift_ref[2], expand_ref[2])
    for i in range(16):
        out_ref[8 + i] = (mean_ref[8 + i].astype(F32) + grown[i]).astype(BF)


def last_outer(
    parity_ref, inner_ref, mean_ref, conv_ref, near_row, far_row, gain_ref, shift_ref, expand_ref,
    out_ref,
):
    odd = jnp.broadcast_to(parity_ref[0], (32, 128)) == 1
    near = [near_row[i].astype(F32) for i in range(8)]
    far = [far_row[i].astype(F32) for i in range(8)]
    sums = [conv_ref[i] + jnp.where(odd, near[i], far[i]) for i in range(8)]
    sums += [conv_ref[8 + i] + jnp.where(odd, far[i], near[i]) for i in range(8)]
    grown = grow(sums, gain_ref[2], shift_ref[2], expand_ref[2])
    out_ref[8:24] = inner_ref[8:24]
    for i in range(16):
        at = i if i < 8 else 16 + i
        out_ref[at] = (mean_ref[at].astype(F32) + grown[i]).astype(BF)


def on_device(contact_map, dilations, conv_weight, conv_gain, conv_shift, out_weight):
    rows, cols = lax.axis_size("row"), lax.axis_size("col")
    row, col = lax.axis_index("row"), lax.axis_index("col")
    mixed = lax.bitwise_xor(lax.rem(row, 4), lax.rem(lax.div(row, 4) + col, 4))
    scalars = jnp.concatenate([dilations, jnp.stack([row, col, mixed]).astype(jnp.int32)])
    parity = jnp.broadcast_to(
        jnp.stack([lax.rem(row, 2), lax.rem(col, 2)]).astype(jnp.int32)[:, None, None], (2, 1, 128)
    )
    near_rows = [(r, r ^ 1) for r in range(rows)]
    far_rows = [(r, r + 1) for r in range(1, rows - 1, 2)]
    far_rows += [(d, r) for r, d in far_rows]
    near_pairs = [(c, c ^ 1) for c in range(cols)]
    far_pairs = [(c, c + 1) for c in range(1, cols - 1, 2)]
    far_pairs += [(d, c) for c, d in far_pairs]

    own = jnp.transpose(contact_map, (1, 0, 2))
    odd_row = lax.rem(row, 2)

    def rim(start):
        return jnp.transpose(lax.dynamic_slice_in_dim(contact_map, start, 16, 1), (1, 0, 2))

    far_row = lax.ppermute(rim(16 * odd_row), "row", far_rows)
    near_row = lax.ppermute(rim(16 - 16 * odd_row), "row", near_rows)
    sides = call(
        pack_sides,
        jax.ShapeDtypeStruct((2, 8, 64, 128), BF),
        (parity, near_row, far_row, own),
        0,
        [],
        0,
        1 << 20,
    )
    far = lax.ppermute(sides[1], "col", far_pairs)
    near = lax.ppermute(sides[0], "col", near_pairs)
    kernel = jnp.transpose(conv_weight.reshape(3, 3, 3, 32, 64), (0, 2, 3, 1, 4)).reshape(3, 96, 192)
    gain = jnp.broadcast_to(conv_gain[:, :, None], (3, 32, 128))
    shift = jnp.broadcast_to(conv_shift[:, :, None], (3, 32, 128))
    weights = (kernel, gain, shift, out_weight)

    tile = jax.ShapeDtypeStruct((32, 64, 128), BF)
    second, messages = call(
        first_blocks,
        (tile, jax.ShapeDtypeStruct((4, 512, 128), BF)),
        (scalars, near_row, own, far_row, near, far, *weights),
        1,
        [
            pltpu.VMEM((64, 64, 256), BF),
            pltpu.VMEM((48, 64, 256), BF),
            pltpu.VMEM((128 * 16, 128), F32),
        ],
        80 * 256 * 64 * 32 * 20,
        4 << 20,
    )
    received = []
    for t in range(4):
        pairs = []
        for a in range(rows // 4):
            for k in range(4):
                for b in range(cols):
                    pairs.append(((4 * a + k) * cols + b, (4 * b + (k ^ t ^ (a + b) % 4)) * cols + a))
        received.append(lax.ppermute(messages[t], BOTH, pairs))
    mean, sides = call(
        average,
        (tile, jax.ShapeDtypeStruct((2, 4, 64, 128), BF)),
        (scalars, second, *received),
        1,
        [pltpu.VMEM((4, 512, 128), BF)],
        0,
        2 << 20,
    )
    far = lax.ppermute(sides[1], "col", far_pairs)
    near = lax.ppermute(sides[0], "col", near_pairs)
    edge = functools.partial(
        call,
        outs=jax.ShapeDtypeStruct((8, 32, 128), BF),
        n_smem=1,
        scratch=[pltpu.VMEM((16, 64, 256), BF)],
        flops=8 * 256 * 64 * 96 * 2,
        moved=1 << 19,
    )
    sources = (scalars, mean, near, far, kernel)
    to_far = edge(functools.partial(last_edge, False), args=sources)
    far_row = lax.ppermute(to_far, "row", far_rows)
    to_near = edge(functools.partial(last_edge, True), args=(*sources, to_far))
    near_row = lax.ppermute(to_near, "row", near_rows)
    inner, conv = call(
        last_inner,
        (tile, jax.ShapeDtypeStruct((16, 32, 128), F32)),
        (scalars, mean, near, far, *weights),
        1,
        [pltpu.VMEM((48, 64, 256), BF)],
        32 * 256 * 64 * 32 * 20,
        2 << 20,
    )
    out = call(
        last_outer,
        tile,
        (parity, inner, mean, conv, near_row, far_row, gain, shift, out_weight),
        0,
        [],
        16 * 256 * 64 * 32 * 2,
        2 << 20,
    )
    return jnp.transpose(out, (1, 0, 2))


def solution(mesh):
    return jax.shard_map(
        on_device,
        mesh=mesh,
        in_specs=(P(None, "row", "col"), P(), P(), P(), P(), P()),
        out_specs=P(None, "row", "col"),
        check_vma=False,
    )
```

```python
import jax
import jax.numpy as jnp
from jax import lax
from jax.experimental import pallas as pl
from jax.experimental.pallas import tpu as pltpu
from jax.sharding import PartitionSpec as P

D = 8
BOTH = ("row", "col")
BF = jnp.bfloat16
F32 = jnp.float32
VMEM = pl.BlockSpec(memory_space=pltpu.VMEM)
SMEM = pl.BlockSpec(memory_space=pltpu.SMEM)
LIMIT = 40 * 1024 * 1024


def call(body, outs, args, n_smem, scratch, flops, moved):
    return pl.pallas_call(
        body,
        out_shape=outs,
        in_specs=[SMEM] * n_smem + [VMEM] * (len(args) - n_smem),
        out_specs=jax.tree.map(lambda _: VMEM, outs),
        scratch_shapes=scratch,
        compiler_params=pltpu.CompilerParams(vmem_limit_bytes=LIMIT),
        cost_estimate=pl.CostEstimate(flops=flops, bytes_accessed=moved, transcendentals=0),
    )(*args)


def lanes(rows):
    return lax.broadcasted_iota(jnp.int32, (rows, 128), 1)


def pack_strips(pieces, start, width):
    lane = lanes(64)
    total = None
    for place, piece in enumerate(pieces):
        moved = pltpu.roll(piece.astype(F32), (place * width - start) % 128, 1)
        total = moved if total is None else jnp.where(lane >= place * width, moved, total)
    return total


def side_lanes(from_right, from_left, place, width):
    lane = lanes(64)
    right = pltpu.roll(from_right.astype(F32), (-place * width) % 128, 1)
    left = pltpu.roll(from_left.astype(F32), (128 - width - place * width) % 128, 1)
    side = jnp.where(lane < width, right, jnp.where(lane >= 128 - width, left, 0.0))
    return side.astype(BF)


def tap_sums(taps, spacing, narrow):
    lane = lanes(32)
    before, after = lane >= spacing, lane < 128 - spacing
    sums = []
    for tap in taps:
        left = [pltpu.roll(tap[:32, h : h + 128], spacing, 1) for h in (0, 128)]
        right = [pltpu.roll(tap[64:, h : h + 128], 128 - spacing, 1) for h in (0, 128)]
        sums.append(
            [
                tap[32:64, 128 * h : 128 * h + 128]
                + jnp.where(before, left[h], left[1 - h])
                + jnp.where(after, right[h], right[1 - h])
                for h in range(1 if narrow else 2)
            ]
        )
    return sums


def conv_rows(source, rows, spacing, kernel, narrow):
    taps = []
    for at in rows:
        stacked = jnp.concatenate(
            [source[at - spacing], source[at], source[at + spacing]], axis=0
        )
        taps.append(jnp.dot(kernel, jnp.maximum(stacked, 0), preferred_element_type=F32))
    return tap_sums(taps, spacing, narrow)


def grow(sums, gain, shift, expand):
    hidden = [jnp.maximum(gain * conv + shift, 0.0).astype(BF) for conv in sums]
    grown = []
    for i in range(0, len(hidden), 2):
        both = jnp.dot(
            expand, jnp.concatenate(hidden[i : i + 2], axis=1), preferred_element_type=F32
        )
        grown += [both[:, :128], both[:, 128:]]
    return grown


def block_rows(source, rows, spacing, kernel, gain, shift, expand, narrow=False):
    sums = conv_rows(source, rows, spacing, kernel, narrow)
    grown = grow([conv for row in sums for conv in row], gain, shift, expand)
    if narrow:
        return [source[at, :, :128].astype(F32) + g for at, g in zip(rows, grown)]
    return [
        source[at].astype(F32) + jnp.concatenate(grown[2 * i : 2 * i + 2], axis=1)
        for i, at in enumerate(rows)
    ]


def block_of(layer, spacing_ref, kernel_ref, gain_ref, shift_ref, expand_ref):
    return (
        spacing_ref[layer], kernel_ref[layer], gain_ref[layer], shift_ref[layer], expand_ref[layer]
    )


def pack_rows(rows, odd, sides_ref):
    for g in range(len(rows) // 8):
        pieces = rows[8 * g : 8 * g + 8]
        left, right = pack_strips(pieces, 0, 16), pack_strips(pieces, 112, 16)
        sides_ref[0, g] = jnp.where(odd, left, right).astype(BF)
        sides_ref[1, g] = jnp.where(odd, right, left).astype(BF)


def pack_sides(parity_ref, near_row, far_row, own_ref, sides_ref):
    odd = jnp.broadcast_to(parity_ref[1], (64, 128)) == 1
    rows = [ref[r] for ref in (near_row, own_ref, far_row) for r in range(ref.shape[0])]
    pack_rows(rows, odd, sides_ref)


def fill_wide(wide, parts, odd_col, near_ref, far_ref):
    for ref, count, source, start, block in parts:
        for r in range(count):
            if r % 8 == 0:
                near, far = near_ref[block + r // 8], far_ref[block + r // 8]
                from_left = jnp.where(odd_col, near, far)
                from_right = jnp.where(odd_col, far, near)
            wide[start + r, :, :128] = ref[source + r]
            wide[start + r, :, 128:] = side_lanes(from_right, from_left, r % 8, 16)


def first_blocks(
    scalar_ref, near_row, own_ref, far_row, near_ref, far_ref,
    kernel_ref, gain_ref, shift_ref, expand_ref,
    second_ref, message_ref, wide, middle, turned,
):
    row, col, members = scalar_ref[3], scalar_ref[4], scalar_ref[5]
    weights = (scalar_ref, kernel_ref, gain_ref, shift_ref, expand_ref)
    far_start = 48 * lax.rem(row, 2)
    parts = (
        (near_row, 16, 0, 48 - far_start, 0),
        (own_ref, 32, 0, 16, 2),
        (far_row, 16, 0, far_start, 6),
    )
    fill_wide(wide, parts, lax.rem(col, 2) == 1, near_ref, far_ref)
    lane = lax.broadcasted_iota(jnp.int32, (64, 256), 1)
    inside = (lane < 128) | ((lane < 192) & (col < 7)) | ((lane >= 192) & (col > 0))

    outs = block_rows(wide, [r + 8 for r in range(48)], *block_of(0, *weights))
    for r, out in enumerate(outs):
        alive = inside
        if not 8 <= r < 40:
            number = 32 * row - 8 + r
            alive = inside & (number >= 0) & (number < 1024)
        middle[r] = jnp.where(alive, out, 0.0).astype(BF)
    rows = [r for b in range(16) for r in (b, b + 16)]
    outs = block_rows(middle, [r + 8 for r in rows], *block_of(1, *weights), narrow=True)
    for r, out in zip(rows, outs):
        second_ref[r] = out.astype(BF)
    for b in range(16):
        pair = jnp.concatenate(outs[2 * b : 2 * b + 2], axis=0).astype(BF)
        turned[pl.ds(b, 128, stride=16), :] = jnp.transpose(pair.astype(F32))
    for m in range(4):
        message_ref[lax.bitwise_xor(members, m)] = turned[512 * m : 512 * m + 512].astype(BF)


def average(scalar_ref, second_ref, m1, m3, m0, m2, mean_ref, sides_ref, gathered):
    members = scalar_ref[5]
    for t, ref in enumerate((m0, m1, m2, m3)):
        gathered[lax.bitwise_xor(members, t)] = ref[...]
    mean = []
    for j in range(32):
        blocks = []
        for k in range(4):
            part = gathered[k, 16 * j : 16 * j + 16, :].astype(F32)
            blocks += [part, pltpu.roll(part, 64, 1)]
        mirrored = jnp.transpose(jnp.concatenate(blocks, axis=0))[:64]
        mean.append((0.5 * (second_ref[j].astype(F32) + mirrored)).astype(BF))
        mean_ref[j] = mean[j]
    pack_rows(mean, lax.rem(scalar_ref[4], 2) == 1, sides_ref)


def edge_taps(up, spacing, wide, first, above, kernel):
    kernel = jnp.where(up == 1, kernel[:, 128:], kernel[:, :64])
    start = jnp.where(up == 1, first - 8 + spacing, above - spacing)
    return [
        jnp.dot(kernel, jnp.maximum(wide[start + i], 0), preferred_element_type=F32)
        for i in range(8)
    ]


def last_far(scalar_ref, mean_ref, near_ref, far_ref, kernel_ref, edge_ref, wide):
    spacing = scalar_ref[2]
    down = lax.rem(scalar_ref[3], 2)
    up = 1 - down
    for r in range(8):
        wide[8 * down + r] = jnp.zeros((64, 256), BF)
    parts = ((mean_ref, 8, 24 * down, 8 * up, 3 * down),)
    fill_wide(wide, parts, lax.rem(scalar_ref[4], 2) == 1, near_ref, far_ref)
    taps = edge_taps(up, spacing, wide, 8, 8, kernel_ref[2])
    for i, conv in enumerate(tap_sums(taps, spacing, True)):
        edge_ref[i] = conv[0].astype(BF)


def last_inner(
    scalar_ref, mean_ref, near_ref, far_ref, kernel_ref, gain_ref, shift_ref, expand_ref,
    out_ref, conv_ref, edge_ref, wide,
):
    for at in range(8):
        wide[at] = jnp.zeros((64, 256), BF)
        wide[40 + at] = jnp.zeros((64, 256), BF)
    parts = ((mean_ref, 32, 0, 8, 0),)
    fill_wide(wide, parts, lax.rem(scalar_ref[4], 2) == 1, near_ref, far_ref)
    spacing = scalar_ref[2]
    taps = edge_taps(lax.rem(scalar_ref[3], 2), spacing, wide, 8, 40, kernel_ref[2])
    edge = tap_sums(taps, spacing, True)
    sums = conv_rows(wide, [r + 8 for r in range(32)], spacing, kernel_ref[2], True)
    sums = [row[0] for row in sums]
    for i in range(8):
        edge_ref[i] = edge[i][0].astype(BF)
        conv_ref[i] = sums[i]
        conv_ref[8 + i] = sums[24 + i]
    grown = grow(sums[8:24], gain_ref[2], shift_ref[2], expand_ref[2])
    for i in range(16):
        out_ref[8 + i] = (mean_ref[8 + i].astype(F32) + grown[i]).astype(BF)


def last_outer(
    parity_ref, inner_ref, mean_ref, conv_ref, near_row, far_row, gain_ref, shift_ref, expand_ref,
    out_ref,
):
    odd = jnp.broadcast_to(parity_ref[0], (32, 128)) == 1
    near = [near_row[i].astype(F32) for i in range(8)]
    far = [far_row[i].astype(F32) for i in range(8)]
    sums = [conv_ref[i] + jnp.where(odd, near[i], far[i]) for i in range(8)]
    sums += [conv_ref[8 + i] + jnp.where(odd, far[i], near[i]) for i in range(8)]
    grown = grow(sums, gain_ref[2], shift_ref[2], expand_ref[2])
    out_ref[8:24] = inner_ref[8:24]
    for i in range(16):
        at = i if i < 8 else 16 + i
        out_ref[at] = (mean_ref[at].astype(F32) + grown[i]).astype(BF)


def on_device(contact_map, dilations, conv_weight, conv_gain, conv_shift, out_weight):
    rows, cols = lax.axis_size("row"), lax.axis_size("col")
    row, col = lax.axis_index("row"), lax.axis_index("col")
    mixed = lax.bitwise_xor(lax.rem(row, 4), lax.rem(lax.div(row, 4) + col, 4))
    scalars = jnp.concatenate([dilations, jnp.stack([row, col, mixed]).astype(jnp.int32)])
    parity = jnp.broadcast_to(
        jnp.stack([lax.rem(row, 2), lax.rem(col, 2)]).astype(jnp.int32)[:, None, None], (2, 1, 128)
    )
    near_rows = [(r, r ^ 1) for r in range(rows)]
    far_rows = [(r, r + 1) for r in range(1, rows - 1, 2)]
    far_rows += [(d, r) for r, d in far_rows]
    near_pairs = [(c, c ^ 1) for c in range(cols)]
    far_pairs = [(c, c + 1) for c in range(1, cols - 1, 2)]
    far_pairs += [(d, c) for c, d in far_pairs]

    own = jnp.transpose(contact_map, (1, 0, 2))
    odd_row = lax.rem(row, 2)

    def rim(start):
        return jnp.transpose(lax.dynamic_slice_in_dim(contact_map, start, 16, 1), (1, 0, 2))

    far_row = lax.ppermute(rim(16 * odd_row), "row", far_rows)
    near_row = lax.ppermute(rim(16 - 16 * odd_row), "row", near_rows)
    sides = call(
        pack_sides,
        jax.ShapeDtypeStruct((2, 8, 64, 128), BF),
        (parity, near_row, far_row, own),
        0,
        [],
        0,
        1 << 20,
    )
    far = lax.ppermute(sides[1], "col", far_pairs)
    near = lax.ppermute(sides[0], "col", near_pairs)
    kernel = jnp.transpose(conv_weight.reshape(3, 3, 3, 32, 64), (0, 2, 3, 1, 4)).reshape(3, 96, 192)
    gain = jnp.broadcast_to(conv_gain[:, :, None], (3, 32, 128))
    shift = jnp.broadcast_to(conv_shift[:, :, None], (3, 32, 128))
    weights = (kernel, gain, shift, out_weight)

    tile = jax.ShapeDtypeStruct((32, 64, 128), BF)
    second, messages = call(
        first_blocks,
        (tile, jax.ShapeDtypeStruct((4, 512, 128), BF)),
        (scalars, near_row, own, far_row, near, far, *weights),
        1,
        [
            pltpu.VMEM((64, 64, 256), BF),
            pltpu.VMEM((48, 64, 256), BF),
            pltpu.VMEM((128 * 16, 128), F32),
        ],
        80 * 256 * 64 * 32 * 20,
        4 << 20,
    )
    received = {}
    for t in (1, 3, 0, 2):
        pairs = []
        for a in range(rows // 4):
            for k in range(4):
                for b in range(cols):
                    pairs.append(((4 * a + k) * cols + b, (4 * b + (k ^ t ^ (a + b) % 4)) * cols + a))
        received[t] = lax.ppermute(messages[t], BOTH, pairs)
    mean, sides = call(
        average,
        (tile, jax.ShapeDtypeStruct((2, 4, 64, 128), BF)),
        (scalars, second, *received.values()),
        1,
        [pltpu.VMEM((4, 512, 128), BF)],
        0,
        2 << 20,
    )
    far = lax.ppermute(sides[1], "col", far_pairs)
    near = lax.ppermute(sides[0], "col", near_pairs)
    edge = jax.ShapeDtypeStruct((8, 32, 128), BF)
    to_far = call(
        last_far,
        edge,
        (scalars, mean, near, far, kernel),
        1,
        [pltpu.VMEM((16, 64, 256), BF)],
        8 * 256 * 64 * 96 * 2,
        1 << 19,
    )
    far_row = lax.ppermute(to_far, "row", far_rows)
    inner, conv, to_near = call(
        last_inner,
        (tile, jax.ShapeDtypeStruct((16, 32, 128), F32), edge),
        (scalars, mean, near, far, *weights),
        1,
        [pltpu.VMEM((48, 64, 256), BF)],
        32 * 256 * 64 * 32 * 20,
        2 << 20,
    )
    near_row = lax.ppermute(to_near, "row", near_rows)
    out = call(
        last_outer,
        tile,
        (parity, inner, mean, conv, near_row, far_row, gain, shift, out_weight),
        0,
        [],
        16 * 256 * 64 * 32 * 2,
        2 << 20,
    )
    return jnp.transpose(out, (1, 0, 2))


def solution(mesh):
    return jax.shard_map(
        on_device,
        mesh=mesh,
        in_specs=(P(None, "row", "col"), P(), P(), P(), P(), P()),
        out_specs=P(None, "row", "col"),
        check_vma=False,
    )
```

```python
import jax
import jax.numpy as jnp
from jax import lax
from jax.experimental import pallas as pl
from jax.experimental.pallas import tpu as pltpu
from jax.sharding import PartitionSpec as P

D = 8
BOTH = ("row", "col")
BF = jnp.bfloat16
F32 = jnp.float32
VMEM = pl.BlockSpec(memory_space=pltpu.VMEM)
SMEM = pl.BlockSpec(memory_space=pltpu.SMEM)
LIMIT = 40 * 1024 * 1024


def call(body, outs, args, n_smem, scratch, flops, moved):
    return pl.pallas_call(
        body,
        out_shape=outs,
        in_specs=[SMEM] * n_smem + [VMEM] * (len(args) - n_smem),
        out_specs=jax.tree.map(lambda _: VMEM, outs),
        scratch_shapes=scratch,
        compiler_params=pltpu.CompilerParams(vmem_limit_bytes=LIMIT),
        cost_estimate=pl.CostEstimate(flops=flops, bytes_accessed=moved, transcendentals=0),
    )(*args)


def lanes(rows):
    return lax.broadcasted_iota(jnp.int32, (rows, 128), 1)


def pack_strips(pieces, start, width):
    lane = lanes(64)
    total = None
    for place, piece in enumerate(pieces):
        moved = pltpu.roll(piece.astype(F32), (place * width - start) % 128, 1)
        total = moved if total is None else jnp.where(lane >= place * width, moved, total)
    return total


def side_lanes(from_right, from_left, place, width):
    lane = lanes(64)
    right = pltpu.roll(from_right.astype(F32), (-place * width) % 128, 1)
    left = pltpu.roll(from_left.astype(F32), (128 - width - place * width) % 128, 1)
    side = jnp.where(lane < width, right, jnp.where(lane >= 128 - width, left, 0.0))
    return side.astype(BF)


def tap_sums(taps, spacing, narrow):
    lane = lanes(32)
    before, after = lane >= spacing, lane < 128 - spacing
    sums = []
    for tap in taps:
        left = [pltpu.roll(tap[:32, h : h + 128], spacing, 1) for h in (0, 128)]
        right = [pltpu.roll(tap[64:, h : h + 128], 128 - spacing, 1) for h in (0, 128)]
        sums.append(
            [
                tap[32:64, 128 * h : 128 * h + 128]
                + jnp.where(before, left[h], left[1 - h])
                + jnp.where(after, right[h], right[1 - h])
                for h in range(1 if narrow else 2)
            ]
        )
    return sums


def conv_rows(source, rows, spacing, kernel, narrow):
    taps = []
    for at in rows:
        stacked = jnp.concatenate(
            [source[at - spacing], source[at], source[at + spacing]], axis=0
        )
        taps.append(jnp.dot(kernel, jnp.maximum(stacked, 0), preferred_element_type=F32))
    return tap_sums(taps, spacing, narrow)


def grow(sums, gain, shift, expand):
    hidden = [jnp.maximum(gain * conv + shift, 0.0).astype(BF) for conv in sums]
    grown = []
    for i in range(0, len(hidden), 2):
        both = jnp.dot(
            expand, jnp.concatenate(hidden[i : i + 2], axis=1), preferred_element_type=F32
        )
        grown += [both[:, :128], both[:, 128:]]
    return grown


def block_rows(source, rows, spacing, kernel, gain, shift, expand, narrow=False):
    sums = conv_rows(source, rows, spacing, kernel, narrow)
    grown = grow([conv for row in sums for conv in row], gain, shift, expand)
    if narrow:
        return [source[at, :, :128].astype(F32) + g for at, g in zip(rows, grown)]
    return [
        source[at].astype(F32) + jnp.concatenate(grown[2 * i : 2 * i + 2], axis=1)
        for i, at in enumerate(rows)
    ]


def block_of(layer, spacing_ref, kernel_ref, gain_ref, shift_ref, expand_ref):
    return (
        spacing_ref[layer], kernel_ref[layer], gain_ref[layer], shift_ref[layer], expand_ref[layer]
    )


def pack_rows(rows, odd, sides_ref):
    for g in range(len(rows) // 8):
        pieces = rows[8 * g : 8 * g + 8]
        left, right = pack_strips(pieces, 0, 16), pack_strips(pieces, 112, 16)
        sides_ref[0, g] = jnp.where(odd, left, right).astype(BF)
        sides_ref[1, g] = jnp.where(odd, right, left).astype(BF)


def pack_sides(parity_ref, near_row, far_row, own_ref, sides_ref):
    odd = jnp.broadcast_to(parity_ref[1], (64, 128)) == 1
    rows = [ref[r] for ref in (near_row, own_ref, far_row) for r in range(ref.shape[0])]
    pack_rows(rows, odd, sides_ref)


def fill_wide(wide, parts, odd_col, near_ref, far_ref):
    for ref, count, source, start, block in parts:
        for r in range(count):
            if r % 8 == 0:
                near, far = near_ref[block + r // 8], far_ref[block + r // 8]
                from_left = jnp.where(odd_col, near, far)
                from_right = jnp.where(odd_col, far, near)
            wide[start + r, :, :128] = ref[source + r]
            wide[start + r, :, 128:] = side_lanes(from_right, from_left, r % 8, 16)


def first_blocks(
    scalar_ref, near_row, own_ref, far_row, near_ref, far_ref,
    kernel_ref, gain_ref, shift_ref, expand_ref,
    second_ref, message_ref, wide, middle, turned,
):
    row, col, members = scalar_ref[3], scalar_ref[4], scalar_ref[5]
    weights = (scalar_ref, kernel_ref, gain_ref, shift_ref, expand_ref)
    far_start = 48 * lax.rem(row, 2)
    parts = (
        (near_row, 16, 0, 48 - far_start, 0),
        (own_ref, 32, 0, 16, 2),
        (far_row, 16, 0, far_start, 6),
    )
    fill_wide(wide, parts, lax.rem(col, 2) == 1, near_ref, far_ref)
    lane = lax.broadcasted_iota(jnp.int32, (64, 256), 1)
    inside = (lane < 128) | ((lane < 192) & (col < 7)) | ((lane >= 192) & (col > 0))

    outs = block_rows(wide, [r + 8 for r in range(48)], *block_of(0, *weights))
    for r, out in enumerate(outs):
        alive = inside
        if not 8 <= r < 40:
            number = 32 * row - 8 + r
            alive = inside & (number >= 0) & (number < 1024)
        middle[r] = jnp.where(alive, out, 0.0).astype(BF)
    rows = [r for b in range(16) for r in (b, b + 16)]
    outs = block_rows(middle, [r + 8 for r in rows], *block_of(1, *weights), narrow=True)
    for r, out in zip(rows, outs):
        second_ref[r] = out.astype(BF)
    for b in range(16):
        pair = jnp.concatenate(outs[2 * b : 2 * b + 2], axis=0).astype(BF)
        turned[pl.ds(b, 128, stride=16), :] = jnp.transpose(pair.astype(F32))
    for m in range(4):
        message_ref[lax.bitwise_xor(members, m)] = turned[512 * m : 512 * m + 512].astype(BF)


def average(scalar_ref, second_ref, m0, m1, m2, m3, mean_ref, sides_ref, gathered):
    members = scalar_ref[5]
    for t, ref in enumerate((m0, m1, m2, m3)):
        gathered[lax.bitwise_xor(members, t)] = ref[...]
    mean = []
    for j in range(32):
        blocks = []
        for k in range(4):
            part = gathered[k, 16 * j : 16 * j + 16, :].astype(F32)
            blocks += [part, pltpu.roll(part, 64, 1)]
        mirrored = jnp.transpose(jnp.concatenate(blocks, axis=0))[:64]
        mean.append((0.5 * (second_ref[j].astype(F32) + mirrored)).astype(BF))
        mean_ref[j] = mean[j]
    pack_rows(mean, lax.rem(scalar_ref[4], 2) == 1, sides_ref)


def edge_rows(mean_ref, scalar_ref, near_ref, far_ref, wide):
    for r in range(8):
        wide[r] = jnp.zeros((64, 256), BF)
        wide[24 + r] = jnp.zeros((64, 256), BF)
    parts = ((mean_ref, 8, 0, 8, 0), (mean_ref, 8, 24, 16, 3))
    fill_wide(wide, parts, lax.rem(scalar_ref[4], 2) == 1, near_ref, far_ref)


def last_edges(
    scalar_ref, mean_ref, near_ref, far_ref, kernel_ref, to_far_ref, to_near_ref, wide
):
    spacing, kernel = scalar_ref[2], kernel_ref[2]
    odd = lax.rem(scalar_ref[3], 2) == 1
    edge_rows(mean_ref, scalar_ref, near_ref, far_ref, wide)
    taps = []
    for i in range(8):
        up = jnp.maximum(wide[i + spacing], 0)
        taps.append(jnp.dot(kernel[:, 128:], up, preferred_element_type=F32))
        down = jnp.maximum(wide[24 + i - spacing], 0)
        taps.append(jnp.dot(kernel[:, :64], down, preferred_element_type=F32))
    sums = tap_sums(taps, spacing, True)
    for i in range(8):
        up, down = sums[2 * i][0], sums[2 * i + 1][0]
        to_far_ref[i] = jnp.where(odd, down, up).astype(BF)
        to_near_ref[i] = jnp.where(odd, up, down).astype(BF)


def last_inner(
    scalar_ref, mean_ref, near_ref, far_ref, kernel_ref, gain_ref, shift_ref, expand_ref,
    out_ref, conv_ref, wide,
):
    for at in range(8):
        wide[at] = jnp.zeros((64, 256), BF)
        wide[40 + at] = jnp.zeros((64, 256), BF)
    parts = ((mean_ref, 32, 0, 8, 0),)
    fill_wide(wide, parts, lax.rem(scalar_ref[4], 2) == 1, near_ref, far_ref)
    sums = conv_rows(wide, [r + 8 for r in range(32)], scalar_ref[2], kernel_ref[2], True)
    sums = [row[0] for row in sums]
    for i in range(8):
        conv_ref[i] = sums[i]
        conv_ref[8 + i] = sums[24 + i]
    grown = grow(sums[8:24], gain_ref[2], shift_ref[2], expand_ref[2])
    for i in range(16):
        out_ref[8 + i] = (mean_ref[8 + i].astype(F32) + grown[i]).astype(BF)


def last_outer(
    parity_ref, inner_ref, mean_ref, conv_ref, far_row, near_row, gain_ref, shift_ref, expand_ref,
    out_ref,
):
    odd = jnp.broadcast_to(parity_ref[0], (32, 128)) == 1
    near = [near_row[i].astype(F32) for i in range(8)]
    far = [far_row[i].astype(F32) for i in range(8)]
    sums = [conv_ref[i] + jnp.where(odd, near[i], far[i]) for i in range(8)]
    sums += [conv_ref[8 + i] + jnp.where(odd, far[i], near[i]) for i in range(8)]
    grown = grow(sums, gain_ref[2], shift_ref[2], expand_ref[2])
    out_ref[8:24] = inner_ref[8:24]
    for i in range(16):
        at = i if i < 8 else 16 + i
        out_ref[at] = (mean_ref[at].astype(F32) + grown[i]).astype(BF)


def on_device(contact_map, dilations, conv_weight, conv_gain, conv_shift, out_weight):
    rows, cols = lax.axis_size("row"), lax.axis_size("col")
    row, col = lax.axis_index("row"), lax.axis_index("col")
    mixed = lax.bitwise_xor(lax.rem(row, 4), lax.rem(lax.div(row, 4) + col, 4))
    scalars = jnp.concatenate([dilations, jnp.stack([row, col, mixed]).astype(jnp.int32)])
    parity = jnp.broadcast_to(
        jnp.stack([lax.rem(row, 2), lax.rem(col, 2)]).astype(jnp.int32)[:, None, None], (2, 1, 128)
    )
    near_rows = [(r, r ^ 1) for r in range(rows)]
    far_rows = [(r, r + 1) for r in range(1, rows - 1, 2)]
    far_rows += [(d, r) for r, d in far_rows]
    near_pairs = [(c, c ^ 1) for c in range(cols)]
    far_pairs = [(c, c + 1) for c in range(1, cols - 1, 2)]
    far_pairs += [(d, c) for c, d in far_pairs]

    own = jnp.transpose(contact_map, (1, 0, 2))
    odd_row = lax.rem(row, 2)

    def rim(start):
        return jnp.transpose(lax.dynamic_slice_in_dim(contact_map, start, 16, 1), (1, 0, 2))

    far_row = lax.ppermute(rim(16 * odd_row), "row", far_rows)
    near_row = lax.ppermute(rim(16 - 16 * odd_row), "row", near_rows)
    sides = call(
        pack_sides,
        jax.ShapeDtypeStruct((2, 8, 64, 128), BF),
        (parity, near_row, far_row, own),
        0,
        [],
        0,
        1 << 20,
    )
    far = lax.ppermute(sides[1], "col", far_pairs)
    near = lax.ppermute(sides[0], "col", near_pairs)
    kernel = jnp.transpose(conv_weight.reshape(3, 3, 3, 32, 64), (0, 2, 3, 1, 4)).reshape(3, 96, 192)
    gain = jnp.broadcast_to(conv_gain[:, :, None], (3, 32, 128))
    shift = jnp.broadcast_to(conv_shift[:, :, None], (3, 32, 128))
    weights = (kernel, gain, shift, out_weight)

    tile = jax.ShapeDtypeStruct((32, 64, 128), BF)
    second, messages = call(
        first_blocks,
        (tile, jax.ShapeDtypeStruct((4, 512, 128), BF)),
        (scalars, near_row, own, far_row, near, far, *weights),
        1,
        [
            pltpu.VMEM((64, 64, 256), BF),
            pltpu.VMEM((48, 64, 256), BF),
            pltpu.VMEM((128 * 16, 128), F32),
        ],
        80 * 256 * 64 * 32 * 20,
        4 << 20,
    )
    received = []
    for t in range(4):
        pairs = []
        for a in range(rows // 4):
            for k in range(4):
                for b in range(cols):
                    pairs.append(((4 * a + k) * cols + b, (4 * b + (k ^ t ^ (a + b) % 4)) * cols + a))
        received.append(lax.ppermute(messages[t], BOTH, pairs))
    mean, sides = call(
        average,
        (tile, jax.ShapeDtypeStruct((2, 4, 64, 128), BF)),
        (scalars, second, *received),
        1,
        [pltpu.VMEM((4, 512, 128), BF)],
        0,
        2 << 20,
    )
    far = lax.ppermute(sides[1], "col", far_pairs)
    near = lax.ppermute(sides[0], "col", near_pairs)
    edge = jax.ShapeDtypeStruct((8, 32, 128), BF)
    to_far, to_near = call(
        last_edges,
        (edge, edge),
        (scalars, mean, near, far, kernel),
        1,
        [pltpu.VMEM((32, 64, 256), BF)],
        16 * 256 * 64 * 96 * 2,
        1 << 19,
    )
    far_row = lax.ppermute(to_far, "row", far_rows)
    near_row = lax.ppermute(to_near, "row", near_rows)
    inner, conv = call(
        last_inner,
        (tile, jax.ShapeDtypeStruct((16, 32, 128), F32)),
        (scalars, mean, near, far, *weights),
        1,
        [pltpu.VMEM((48, 64, 256), BF)],
        32 * 256 * 64 * 32 * 20,
        2 << 20,
    )
    out = call(
        last_outer,
        tile,
        (parity, inner, mean, conv, far_row, near_row, gain, shift, out_weight),
        0,
        [],
        16 * 256 * 64 * 32 * 2,
        2 << 20,
    )
    return jnp.transpose(out, (1, 0, 2))


def solution(mesh):
    return jax.shard_map(
        on_device,
        mesh=mesh,
        in_specs=(P(None, "row", "col"), P(), P(), P(), P(), P()),
        out_specs=P(None, "row", "col"),
        check_vma=False,
    )
```

```python
import jax
import jax.numpy as jnp
from jax import lax
from jax.experimental import pallas as pl
from jax.experimental.pallas import tpu as pltpu
from jax.sharding import PartitionSpec as P

D = 8
BOTH = ("row", "col")
BF = jnp.bfloat16
F32 = jnp.float32
VMEM = pl.BlockSpec(memory_space=pltpu.VMEM)
SMEM = pl.BlockSpec(memory_space=pltpu.SMEM)
LIMIT = 40 * 1024 * 1024


def call(body, outs, args, n_smem, scratch, flops, moved):
    return pl.pallas_call(
        body,
        out_shape=outs,
        in_specs=[SMEM] * n_smem + [VMEM] * (len(args) - n_smem),
        out_specs=jax.tree.map(lambda _: VMEM, outs),
        scratch_shapes=scratch,
        compiler_params=pltpu.CompilerParams(vmem_limit_bytes=LIMIT),
        cost_estimate=pl.CostEstimate(flops=flops, bytes_accessed=moved, transcendentals=0),
    )(*args)


def lanes(rows):
    return lax.broadcasted_iota(jnp.int32, (rows, 128), 1)


def pack_strips(pieces, start, width):
    lane = lanes(64)
    total = None
    for place, piece in enumerate(pieces):
        moved = pltpu.roll(piece.astype(F32), (place * width - start) % 128, 1)
        total = moved if total is None else jnp.where(lane >= place * width, moved, total)
    return total


def side_lanes(from_right, from_left, place, width):
    lane = lanes(64)
    right = pltpu.roll(from_right.astype(F32), (-place * width) % 128, 1)
    left = pltpu.roll(from_left.astype(F32), (128 - width - place * width) % 128, 1)
    side = jnp.where(lane < width, right, jnp.where(lane >= 128 - width, left, 0.0))
    return side.astype(BF)


def tap_sums(taps, spacing, narrow):
    lane = lanes(32)
    before, after = lane >= spacing, lane < 128 - spacing
    sums = []
    for tap in taps:
        left = [pltpu.roll(tap[:32, h : h + 128], spacing, 1) for h in (0, 128)]
        right = [pltpu.roll(tap[64:, h : h + 128], 128 - spacing, 1) for h in (0, 128)]
        sums.append(
            [
                tap[32:64, 128 * h : 128 * h + 128]
                + jnp.where(before, left[h], left[1 - h])
                + jnp.where(after, right[h], right[1 - h])
                for h in range(1 if narrow else 2)
            ]
        )
    return sums


def conv_rows(source, rows, spacing, kernel, narrow):
    taps = []
    for at in rows:
        stacked = jnp.concatenate(
            [source[at - spacing], source[at], source[at + spacing]], axis=0
        )
        taps.append(jnp.dot(kernel, jnp.maximum(stacked, 0), preferred_element_type=F32))
    return tap_sums(taps, spacing, narrow)


def grow(sums, gain, shift, expand):
    hidden = [jnp.maximum(gain * conv + shift, 0.0).astype(BF) for conv in sums]
    grown = []
    for i in range(0, len(hidden), 2):
        both = jnp.dot(
            expand, jnp.concatenate(hidden[i : i + 2], axis=1), preferred_element_type=F32
        )
        grown += [both[:, :128], both[:, 128:]]
    return grown


def block_rows(source, rows, spacing, kernel, gain, shift, expand, narrow=False):
    sums = conv_rows(source, rows, spacing, kernel, narrow)
    grown = grow([conv for row in sums for conv in row], gain, shift, expand)
    if narrow:
        return [source[at, :, :128].astype(F32) + g for at, g in zip(rows, grown)]
    return [
        source[at].astype(F32) + jnp.concatenate(grown[2 * i : 2 * i + 2], axis=1)
        for i, at in enumerate(rows)
    ]


def block_of(layer, spacing_ref, kernel_ref, gain_ref, shift_ref, expand_ref):
    return (
        spacing_ref[layer], kernel_ref[layer], gain_ref[layer], shift_ref[layer], expand_ref[layer]
    )


def pack_rows(rows, odd, sides_ref):
    for g in range(len(rows) // 8):
        pieces = rows[8 * g : 8 * g + 8]
        left, right = pack_strips(pieces, 0, 16), pack_strips(pieces, 112, 16)
        sides_ref[0, g] = jnp.where(odd, left, right).astype(BF)
        sides_ref[1, g] = jnp.where(odd, right, left).astype(BF)


def pack_sides(parity_ref, near_row, far_row, own_ref, sides_ref):
    odd = jnp.broadcast_to(parity_ref[1], (64, 128)) == 1
    rows = [ref[r] for ref in (near_row, own_ref, far_row) for r in range(ref.shape[0])]
    pack_rows(rows, odd, sides_ref)


def fill_wide(wide, parts, odd_col, near_ref, far_ref):
    for ref, count, source, start, block in parts:
        for r in range(count):
            if r % 8 == 0:
                near, far = near_ref[block + r // 8], far_ref[block + r // 8]
                from_left = jnp.where(odd_col, near, far)
                from_right = jnp.where(odd_col, far, near)
            wide[start + r, :, :128] = ref[source + r]
            wide[start + r, :, 128:] = side_lanes(from_right, from_left, r % 8, 16)


def first_blocks(
    scalar_ref, near_row, own_ref, far_row, near_ref, far_ref,
    kernel_ref, gain_ref, shift_ref, expand_ref,
    second_ref, message_ref, wide, middle, turned,
):
    row, col, members = scalar_ref[3], scalar_ref[4], scalar_ref[5]
    weights = (scalar_ref, kernel_ref, gain_ref, shift_ref, expand_ref)
    far_start = 48 * lax.rem(row, 2)
    parts = (
        (near_row, 16, 0, 48 - far_start, 0),
        (own_ref, 32, 0, 16, 2),
        (far_row, 16, 0, far_start, 6),
    )
    fill_wide(wide, parts, lax.rem(col, 2) == 1, near_ref, far_ref)
    lane = lax.broadcasted_iota(jnp.int32, (64, 256), 1)
    inside = (lane < 128) | ((lane < 192) & (col < 7)) | ((lane >= 192) & (col > 0))

    outs = block_rows(wide, [r + 8 for r in range(48)], *block_of(0, *weights))
    for r, out in enumerate(outs):
        alive = inside
        if not 8 <= r < 40:
            number = 32 * row - 8 + r
            alive = inside & (number >= 0) & (number < 1024)
        middle[r] = jnp.where(alive, out, 0.0).astype(BF)
    rows = [r for b in range(16) for r in (b, b + 16)]
    outs = block_rows(middle, [r + 8 for r in rows], *block_of(1, *weights), narrow=True)
    for r, out in zip(rows, outs):
        second_ref[r] = out.astype(BF)
    for b in range(16):
        pair = jnp.concatenate(outs[2 * b : 2 * b + 2], axis=0).astype(BF)
        turned[pl.ds(b, 128, stride=16), :] = jnp.transpose(pair.astype(F32))
    for m in range(4):
        message_ref[lax.bitwise_xor(members, m)] = turned[512 * m : 512 * m + 512].astype(BF)


def average(scalar_ref, second_ref, m0, m1, m2, m3, mean_ref, sides_ref, gathered):
    members = scalar_ref[5]
    for t, ref in enumerate((m0, m1, m2, m3)):
        gathered[lax.bitwise_xor(members, t)] = ref[...]
    mean = []
    for j in range(32):
        blocks = []
        for k in range(4):
            part = gathered[k, 16 * j : 16 * j + 16, :].astype(F32)
            blocks += [part, pltpu.roll(part, 64, 1)]
        mirrored = jnp.transpose(jnp.concatenate(blocks, axis=0))[:64]
        mean.append((0.5 * (second_ref[j].astype(F32) + mirrored)).astype(BF))
        mean_ref[j] = mean[j]
    pack_rows(mean, lax.rem(scalar_ref[4], 2) == 1, sides_ref)


def edge_rows(mean_ref, scalar_ref, near_ref, far_ref, wide):
    for r in range(8):
        wide[r] = jnp.zeros((64, 256), BF)
        wide[24 + r] = jnp.zeros((64, 256), BF)
    parts = ((mean_ref, 8, 0, 8, 0), (mean_ref, 8, 24, 16, 3))
    fill_wide(wide, parts, lax.rem(scalar_ref[4], 2) == 1, near_ref, far_ref)


def last_edges(
    scalar_ref, mean_ref, near_ref, far_ref, kernel_ref, edges_ref, wide
):
    spacing, kernel = scalar_ref[2], kernel_ref[2]
    odd = lax.rem(scalar_ref[3], 2) == 1
    edge_rows(mean_ref, scalar_ref, near_ref, far_ref, wide)
    taps = []
    for i in range(8):
        up = jnp.maximum(wide[i + spacing], 0)
        taps.append(jnp.dot(kernel[:, 128:], up, preferred_element_type=F32))
        down = jnp.maximum(wide[24 + i - spacing], 0)
        taps.append(jnp.dot(kernel[:, :64], down, preferred_element_type=F32))
    sums = tap_sums(taps, spacing, True)
    for i in range(8):
        up, down = sums[2 * i][0], sums[2 * i + 1][0]
        edges_ref[0, i] = jnp.where(odd, up, down).astype(BF)
        edges_ref[1, i] = jnp.where(odd, down, up).astype(BF)


def last_inner(
    scalar_ref, mean_ref, near_ref, far_ref, kernel_ref, gain_ref, shift_ref, expand_ref,
    out_ref, conv_ref, wide,
):
    for at in range(8):
        wide[at] = jnp.zeros((64, 256), BF)
        wide[40 + at] = jnp.zeros((64, 256), BF)
    parts = ((mean_ref, 32, 0, 8, 0),)
    fill_wide(wide, parts, lax.rem(scalar_ref[4], 2) == 1, near_ref, far_ref)
    sums = conv_rows(wide, [r + 8 for r in range(32)], scalar_ref[2], kernel_ref[2], True)
    sums = [row[0] for row in sums]
    for i in range(8):
        conv_ref[i] = sums[i]
        conv_ref[8 + i] = sums[24 + i]
    grown = grow(sums[8:24], gain_ref[2], shift_ref[2], expand_ref[2])
    for i in range(16):
        out_ref[8 + i] = (mean_ref[8 + i].astype(F32) + grown[i]).astype(BF)


def last_outer(
    parity_ref, inner_ref, mean_ref, conv_ref, near_rows, far_row, gain_ref, shift_ref, expand_ref,
    out_ref,
):
    odd = jnp.broadcast_to(parity_ref[0], (32, 128)) == 1
    near = [near_rows[0, i].astype(F32) for i in range(8)]
    far = [far_row[i].astype(F32) for i in range(8)]
    sums = [conv_ref[i] + jnp.where(odd, near[i], far[i]) for i in range(8)]
    sums += [conv_ref[8 + i] + jnp.where(odd, far[i], near[i]) for i in range(8)]
    grown = grow(sums, gain_ref[2], shift_ref[2], expand_ref[2])
    out_ref[8:24] = inner_ref[8:24]
    for i in range(16):
        at = i if i < 8 else 16 + i
        out_ref[at] = (mean_ref[at].astype(F32) + grown[i]).astype(BF)


def on_device(contact_map, dilations, conv_weight, conv_gain, conv_shift, out_weight):
    rows, cols = lax.axis_size("row"), lax.axis_size("col")
    row, col = lax.axis_index("row"), lax.axis_index("col")
    mixed = lax.bitwise_xor(lax.rem(row, 4), lax.rem(lax.div(row, 4) + col, 4))
    scalars = jnp.concatenate([dilations, jnp.stack([row, col, mixed]).astype(jnp.int32)])
    parity = jnp.broadcast_to(
        jnp.stack([lax.rem(row, 2), lax.rem(col, 2)]).astype(jnp.int32)[:, None, None], (2, 1, 128)
    )
    near_rows = [(r, r ^ 1) for r in range(rows)]
    far_rows = [(r, r + 1) for r in range(1, rows - 1, 2)]
    far_rows += [(d, r) for r, d in far_rows]
    two_rows = [(r, r + 2) for r in range(0, rows - 2, 2)]
    two_rows += [(r, r - 2) for r in range(3, rows, 2)]
    near_pairs = [(c, c ^ 1) for c in range(cols)]
    far_pairs = [(c, c + 1) for c in range(1, cols - 1, 2)]
    far_pairs += [(d, c) for c, d in far_pairs]

    own = jnp.transpose(contact_map, (1, 0, 2))
    odd_row = lax.rem(row, 2)

    def rim(start):
        return jnp.transpose(lax.dynamic_slice_in_dim(contact_map, start, 16, 1), (1, 0, 2))

    far_row = lax.ppermute(rim(16 * odd_row), "row", far_rows)
    near_row = lax.ppermute(rim(16 - 16 * odd_row), "row", near_rows)
    sides = call(
        pack_sides,
        jax.ShapeDtypeStruct((2, 8, 64, 128), BF),
        (parity, near_row, far_row, own),
        0,
        [],
        0,
        1 << 20,
    )
    far = lax.ppermute(sides[1], "col", far_pairs)
    near = lax.ppermute(sides[0], "col", near_pairs)
    kernel = jnp.transpose(conv_weight.reshape(3, 3, 3, 32, 64), (0, 2, 3, 1, 4)).reshape(3, 96, 192)
    gain = jnp.broadcast_to(conv_gain[:, :, None], (3, 32, 128))
    shift = jnp.broadcast_to(conv_shift[:, :, None], (3, 32, 128))
    weights = (kernel, gain, shift, out_weight)

    tile = jax.ShapeDtypeStruct((32, 64, 128), BF)
    second, messages = call(
        first_blocks,
        (tile, jax.ShapeDtypeStruct((4, 512, 128), BF)),
        (scalars, near_row, own, far_row, near, far, *weights),
        1,
        [
            pltpu.VMEM((64, 64, 256), BF),
            pltpu.VMEM((48, 64, 256), BF),
            pltpu.VMEM((128 * 16, 128), F32),
        ],
        80 * 256 * 64 * 32 * 20,
        4 << 20,
    )
    received = []
    for t in range(4):
        pairs = []
        for a in range(rows // 4):
            for k in range(4):
                for b in range(cols):
                    pairs.append(((4 * a + k) * cols + b, (4 * b + (k ^ t ^ (a + b) % 4)) * cols + a))
        received.append(lax.ppermute(messages[t], BOTH, pairs))
    mean, sides = call(
        average,
        (tile, jax.ShapeDtypeStruct((2, 4, 64, 128), BF)),
        (scalars, second, *received),
        1,
        [pltpu.VMEM((4, 512, 128), BF)],
        0,
        2 << 20,
    )
    far = lax.ppermute(sides[1], "col", far_pairs)
    near = lax.ppermute(sides[0], "col", near_pairs)
    edges = call(
        last_edges,
        jax.ShapeDtypeStruct((2, 8, 32, 128), BF),
        (scalars, mean, near, far, kernel),
        1,
        [pltpu.VMEM((32, 64, 256), BF)],
        16 * 256 * 64 * 96 * 2,
        1 << 19,
    )
    swapped = lax.ppermute(edges, "row", near_rows)
    far_row = lax.ppermute(swapped[1], "row", two_rows)
    inner, conv = call(
        last_inner,
        (tile, jax.ShapeDtypeStruct((16, 32, 128), F32)),
        (scalars, mean, near, far, *weights),
        1,
        [pltpu.VMEM((48, 64, 256), BF)],
        32 * 256 * 64 * 32 * 20,
        2 << 20,
    )
    out = call(
        last_outer,
        tile,
        (parity, inner, mean, conv, swapped, far_row, gain, shift, out_weight),
        0,
        [],
        16 * 256 * 64 * 32 * 2,
        2 << 20,
    )
    return jnp.transpose(out, (1, 0, 2))


def solution(mesh):
    return jax.shard_map(
        on_device,
        mesh=mesh,
        in_specs=(P(None, "row", "col"), P(), P(), P(), P(), P()),
        out_specs=P(None, "row", "col"),
        check_vma=False,
    )
```

```python
import jax
import jax.numpy as jnp
from jax import lax
from jax.experimental import pallas as pl
from jax.experimental.pallas import tpu as pltpu
from jax.sharding import PartitionSpec as P

D = 8
BOTH = ("row", "col")
BF = jnp.bfloat16
F32 = jnp.float32
VMEM = pl.BlockSpec(memory_space=pltpu.VMEM)
SMEM = pl.BlockSpec(memory_space=pltpu.SMEM)
LIMIT = 40 * 1024 * 1024


def call(body, outs, args, n_smem, scratch, flops, moved):
    return pl.pallas_call(
        body,
        out_shape=outs,
        in_specs=[SMEM] * n_smem + [VMEM] * (len(args) - n_smem),
        out_specs=jax.tree.map(lambda _: VMEM, outs),
        scratch_shapes=scratch,
        compiler_params=pltpu.CompilerParams(vmem_limit_bytes=LIMIT),
        cost_estimate=pl.CostEstimate(flops=flops, bytes_accessed=moved, transcendentals=0),
    )(*args)


def lanes(rows):
    return lax.broadcasted_iota(jnp.int32, (rows, 128), 1)


def pack_strips(pieces, start, width):
    lane = lanes(64)
    total = None
    for place, piece in enumerate(pieces):
        moved = pltpu.roll(piece.astype(F32), (place * width - start) % 128, 1)
        total = moved if total is None else jnp.where(lane >= place * width, moved, total)
    return total


def side_lanes(from_right, from_left, place, width):
    lane = lanes(64)
    right = pltpu.roll(from_right.astype(F32), (-place * width) % 128, 1)
    left = pltpu.roll(from_left.astype(F32), (128 - width - place * width) % 128, 1)
    side = jnp.where(lane < width, right, jnp.where(lane >= 128 - width, left, 0.0))
    return side.astype(BF)


def tap_sums(taps, spacing, narrow):
    lane = lanes(32)
    before, after = lane >= spacing, lane < 128 - spacing
    sums = []
    for tap in taps:
        left = [pltpu.roll(tap[:32, h : h + 128], spacing, 1) for h in (0, 128)]
        right = [pltpu.roll(tap[64:, h : h + 128], 128 - spacing, 1) for h in (0, 128)]
        sums.append(
            [
                tap[32:64, 128 * h : 128 * h + 128]
                + jnp.where(before, left[h], left[1 - h])
                + jnp.where(after, right[h], right[1 - h])
                for h in range(1 if narrow else 2)
            ]
        )
    return sums


def conv_rows(source, rows, spacing, kernel, narrow):
    taps = []
    for at in rows:
        stacked = jnp.concatenate(
            [source[at - spacing], source[at], source[at + spacing]], axis=0
        )
        taps.append(jnp.dot(kernel, jnp.maximum(stacked, 0), preferred_element_type=F32))
    return tap_sums(taps, spacing, narrow)


def grow(sums, gain, shift, expand):
    hidden = [jnp.maximum(gain * conv + shift, 0.0).astype(BF) for conv in sums]
    grown = []
    for i in range(0, len(hidden), 2):
        both = jnp.dot(
            expand, jnp.concatenate(hidden[i : i + 2], axis=1), preferred_element_type=F32
        )
        grown += [both[:, :128], both[:, 128:]]
    return grown


def block_rows(source, rows, spacing, kernel, gain, shift, expand, narrow=False):
    sums = conv_rows(source, rows, spacing, kernel, narrow)
    grown = grow([conv for row in sums for conv in row], gain, shift, expand)
    if narrow:
        return [source[at, :, :128].astype(F32) + g for at, g in zip(rows, grown)]
    return [
        source[at].astype(F32) + jnp.concatenate(grown[2 * i : 2 * i + 2], axis=1)
        for i, at in enumerate(rows)
    ]


def block_of(layer, spacing_ref, kernel_ref, gain_ref, shift_ref, expand_ref):
    return (
        spacing_ref[layer], kernel_ref[layer], gain_ref[layer], shift_ref[layer], expand_ref[layer]
    )


def pack_rows(rows, odd, sides_ref):
    for g in range(len(rows) // 8):
        pieces = rows[8 * g : 8 * g + 8]
        left, right = pack_strips(pieces, 0, 16), pack_strips(pieces, 112, 16)
        sides_ref[0, g] = jnp.where(odd, left, right).astype(BF)
        sides_ref[1, g] = jnp.where(odd, right, left).astype(BF)


def pack_sides(parity_ref, near_row, far_row, own_ref, sides_ref):
    odd = jnp.broadcast_to(parity_ref[1], (64, 128)) == 1
    rows = [ref[r] for ref in (near_row, own_ref, far_row) for r in range(ref.shape[0])]
    pack_rows(rows, odd, sides_ref)


def fill_wide(wide, parts, odd_col, near_ref, far_ref):
    for ref, count, source, start, block in parts:
        for r in range(count):
            if r % 8 == 0:
                near, far = near_ref[block + r // 8], far_ref[block + r // 8]
                from_left = jnp.where(odd_col, near, far)
                from_right = jnp.where(odd_col, far, near)
            wide[start + r, :, :128] = ref[source + r]
            wide[start + r, :, 128:] = side_lanes(from_right, from_left, r % 8, 16)


def first_blocks(
    scalar_ref, near_row, own_ref, far_row, near_ref, far_ref,
    kernel_ref, gain_ref, shift_ref, expand_ref,
    second_ref, message_ref, wide, middle, turned,
):
    row, col, members = scalar_ref[3], scalar_ref[4], scalar_ref[5]
    weights = (scalar_ref, kernel_ref, gain_ref, shift_ref, expand_ref)
    far_start = 48 * lax.rem(row, 2)
    parts = (
        (near_row, 16, 0, 48 - far_start, 0),
        (own_ref, 32, 0, 16, 2),
        (far_row, 16, 0, far_start, 6),
    )
    fill_wide(wide, parts, lax.rem(col, 2) == 1, near_ref, far_ref)
    lane = lax.broadcasted_iota(jnp.int32, (64, 256), 1)
    inside = (lane < 128) | ((lane < 192) & (col < 7)) | ((lane >= 192) & (col > 0))

    outs = block_rows(wide, [r + 8 for r in range(48)], *block_of(0, *weights))
    for r, out in enumerate(outs):
        alive = inside
        if not 8 <= r < 40:
            number = 32 * row - 8 + r
            alive = inside & (number >= 0) & (number < 1024)
        middle[r] = jnp.where(alive, out, 0.0).astype(BF)
    rows = [r for b in range(16) for r in (b, b + 16)]
    outs = block_rows(middle, [r + 8 for r in rows], *block_of(1, *weights), narrow=True)
    for r, out in zip(rows, outs):
        second_ref[r] = out.astype(BF)
    for b in range(16):
        pair = jnp.concatenate(outs[2 * b : 2 * b + 2], axis=0).astype(BF)
        turned[pl.ds(b, 128, stride=16), :] = jnp.transpose(pair.astype(F32))
    for m in range(4):
        message_ref[lax.bitwise_xor(members, m)] = turned[512 * m : 512 * m + 512].astype(BF)


def average(scalar_ref, second_ref, m0, m2, m1, m3, mean_ref, sides_ref, gathered):
    members = scalar_ref[5]
    for t, ref in enumerate((m0, m1, m2, m3)):
        gathered[lax.bitwise_xor(members, t)] = ref[...]
    mean = []
    for j in range(32):
        blocks = []
        for k in range(4):
            part = gathered[k, 16 * j : 16 * j + 16, :].astype(F32)
            blocks += [part, pltpu.roll(part, 64, 1)]
        mirrored = jnp.transpose(jnp.concatenate(blocks, axis=0))[:64]
        mean.append((0.5 * (second_ref[j].astype(F32) + mirrored)).astype(BF))
        mean_ref[j] = mean[j]
    pack_rows(mean, lax.rem(scalar_ref[4], 2) == 1, sides_ref)


def edge_rows(mean_ref, scalar_ref, near_ref, far_ref, wide):
    for r in range(8):
        wide[r] = jnp.zeros((64, 256), BF)
        wide[24 + r] = jnp.zeros((64, 256), BF)
    parts = ((mean_ref, 8, 0, 8, 0), (mean_ref, 8, 24, 16, 3))
    fill_wide(wide, parts, lax.rem(scalar_ref[4], 2) == 1, near_ref, far_ref)


def last_edges(
    scalar_ref, mean_ref, near_ref, far_ref, kernel_ref, to_far_ref, to_near_ref, wide
):
    spacing, kernel = scalar_ref[2], kernel_ref[2]
    odd = lax.rem(scalar_ref[3], 2) == 1
    edge_rows(mean_ref, scalar_ref, near_ref, far_ref, wide)
    taps = []
    for i in range(8):
        up = jnp.maximum(wide[i + spacing], 0)
        taps.append(jnp.dot(kernel[:, 128:], up, preferred_element_type=F32))
        down = jnp.maximum(wide[24 + i - spacing], 0)
        taps.append(jnp.dot(kernel[:, :64], down, preferred_element_type=F32))
    sums = tap_sums(taps, spacing, True)
    for i in range(8):
        up, down = sums[2 * i][0], sums[2 * i + 1][0]
        to_far_ref[i] = jnp.where(odd, down, up).astype(BF)
        to_near_ref[i] = jnp.where(odd, up, down).astype(BF)


def last_inner(
    scalar_ref, mean_ref, near_ref, far_ref, kernel_ref, gain_ref, shift_ref, expand_ref,
    out_ref, conv_ref, wide,
):
    for at in range(8):
        wide[at] = jnp.zeros((64, 256), BF)
        wide[40 + at] = jnp.zeros((64, 256), BF)
    parts = ((mean_ref, 32, 0, 8, 0),)
    fill_wide(wide, parts, lax.rem(scalar_ref[4], 2) == 1, near_ref, far_ref)
    sums = conv_rows(wide, [r + 8 for r in range(32)], scalar_ref[2], kernel_ref[2], True)
    sums = [row[0] for row in sums]
    for i in range(8):
        conv_ref[i] = sums[i]
        conv_ref[8 + i] = sums[24 + i]
    grown = grow(sums[8:24], gain_ref[2], shift_ref[2], expand_ref[2])
    for i in range(16):
        out_ref[8 + i] = (mean_ref[8 + i].astype(F32) + grown[i]).astype(BF)


def last_outer(
    parity_ref, inner_ref, mean_ref, conv_ref, far_row, near_row, gain_ref, shift_ref, expand_ref,
    out_ref,
):
    odd = jnp.broadcast_to(parity_ref[0], (32, 128)) == 1
    near = [near_row[i].astype(F32) for i in range(8)]
    far = [far_row[i].astype(F32) for i in range(8)]
    sums = [conv_ref[i] + jnp.where(odd, near[i], far[i]) for i in range(8)]
    sums += [conv_ref[8 + i] + jnp.where(odd, far[i], near[i]) for i in range(8)]
    grown = grow(sums, gain_ref[2], shift_ref[2], expand_ref[2])
    out_ref[8:24] = inner_ref[8:24]
    for i in range(16):
        at = i if i < 8 else 16 + i
        out_ref[at] = (mean_ref[at].astype(F32) + grown[i]).astype(BF)


def on_device(contact_map, dilations, conv_weight, conv_gain, conv_shift, out_weight):
    rows, cols = lax.axis_size("row"), lax.axis_size("col")
    row, col = lax.axis_index("row"), lax.axis_index("col")
    mixed = lax.bitwise_xor(lax.rem(row, 4), lax.rem(lax.div(row, 4) + col, 4))
    scalars = jnp.concatenate([dilations, jnp.stack([row, col, mixed]).astype(jnp.int32)])
    parity = jnp.broadcast_to(
        jnp.stack([lax.rem(row, 2), lax.rem(col, 2)]).astype(jnp.int32)[:, None, None], (2, 1, 128)
    )
    near_rows = [(r, r ^ 1) for r in range(rows)]
    far_rows = [(r, r + 1) for r in range(1, rows - 1, 2)]
    far_rows += [(d, r) for r, d in far_rows]
    near_pairs = [(c, c ^ 1) for c in range(cols)]
    far_pairs = [(c, c + 1) for c in range(1, cols - 1, 2)]
    far_pairs += [(d, c) for c, d in far_pairs]

    own = jnp.transpose(contact_map, (1, 0, 2))
    odd_row = lax.rem(row, 2)

    def rim(start):
        return jnp.transpose(lax.dynamic_slice_in_dim(contact_map, start, 16, 1), (1, 0, 2))

    far_row = lax.ppermute(rim(16 * odd_row), "row", far_rows)
    near_row = lax.ppermute(rim(16 - 16 * odd_row), "row", near_rows)
    sides = call(
        pack_sides,
        jax.ShapeDtypeStruct((2, 8, 64, 128), BF),
        (parity, near_row, far_row, own),
        0,
        [],
        0,
        1 << 20,
    )
    far = lax.ppermute(sides[1], "col", far_pairs)
    near = lax.ppermute(sides[0], "col", near_pairs)
    kernel = jnp.transpose(conv_weight.reshape(3, 3, 3, 32, 64), (0, 2, 3, 1, 4)).reshape(3, 96, 192)
    gain = jnp.broadcast_to(conv_gain[:, :, None], (3, 32, 128))
    shift = jnp.broadcast_to(conv_shift[:, :, None], (3, 32, 128))
    weights = (kernel, gain, shift, out_weight)

    tile = jax.ShapeDtypeStruct((32, 64, 128), BF)
    second, messages = call(
        first_blocks,
        (tile, jax.ShapeDtypeStruct((4, 512, 128), BF)),
        (scalars, near_row, own, far_row, near, far, *weights),
        1,
        [
            pltpu.VMEM((64, 64, 256), BF),
            pltpu.VMEM((48, 64, 256), BF),
            pltpu.VMEM((128 * 16, 128), F32),
        ],
        80 * 256 * 64 * 32 * 20,
        4 << 20,
    )
    received = []
    for t in range(4):
        pairs = []
        for a in range(rows // 4):
            for k in range(4):
                for b in range(cols):
                    pairs.append(((4 * a + k) * cols + b, (4 * b + (k ^ t ^ (a + b) % 4)) * cols + a))
        received.append(lax.ppermute(messages[t], BOTH, pairs))
    mean, sides = call(
        average,
        (tile, jax.ShapeDtypeStruct((2, 4, 64, 128), BF)),
        (scalars, second, received[0], received[2], received[1], received[3]),
        1,
        [pltpu.VMEM((4, 512, 128), BF)],
        0,
        2 << 20,
    )
    far = lax.ppermute(sides[1], "col", far_pairs)
    near = lax.ppermute(sides[0], "col", near_pairs)
    edge = jax.ShapeDtypeStruct((8, 32, 128), BF)
    to_far, to_near = call(
        last_edges,
        (edge, edge),
        (scalars, mean, near, far, kernel),
        1,
        [pltpu.VMEM((32, 64, 256), BF)],
        16 * 256 * 64 * 96 * 2,
        1 << 19,
    )
    far_row = lax.ppermute(to_far, "row", far_rows)
    near_row = lax.ppermute(to_near, "row", near_rows)
    inner, conv = call(
        last_inner,
        (tile, jax.ShapeDtypeStruct((16, 32, 128), F32)),
        (scalars, mean, near, far, *weights),
        1,
        [pltpu.VMEM((48, 64, 256), BF)],
        32 * 256 * 64 * 32 * 20,
        2 << 20,
    )
    out = call(
        last_outer,
        tile,
        (parity, inner, mean, conv, far_row, near_row, gain, shift, out_weight),
        0,
        [],
        16 * 256 * 64 * 32 * 2,
        2 << 20,
    )
    return jnp.transpose(out, (1, 0, 2))


def solution(mesh):
    return jax.shard_map(
        on_device,
        mesh=mesh,
        in_specs=(P(None, "row", "col"), P(), P(), P(), P(), P()),
        out_specs=P(None, "row", "col"),
        check_vma=False,
    )
```

```python
import jax
import jax.numpy as jnp
from jax import lax
from jax.experimental import pallas as pl
from jax.experimental.pallas import tpu as pltpu
from jax.sharding import PartitionSpec as P

D = 8
BOTH = ("row", "col")
BF = jnp.bfloat16
F32 = jnp.float32
VMEM = pl.BlockSpec(memory_space=pltpu.VMEM)
SMEM = pl.BlockSpec(memory_space=pltpu.SMEM)
LIMIT = 40 * 1024 * 1024


def call(body, outs, args, n_smem, scratch, flops, moved):
    return pl.pallas_call(
        body,
        out_shape=outs,
        in_specs=[SMEM] * n_smem + [VMEM] * (len(args) - n_smem),
        out_specs=jax.tree.map(lambda _: VMEM, outs),
        scratch_shapes=scratch,
        compiler_params=pltpu.CompilerParams(vmem_limit_bytes=LIMIT),
        cost_estimate=pl.CostEstimate(flops=flops, bytes_accessed=moved, transcendentals=0),
    )(*args)


def lanes(rows):
    return lax.broadcasted_iota(jnp.int32, (rows, 128), 1)


def pack_strips(pieces, start, width):
    lane = lanes(64)
    total = None
    for place, piece in enumerate(pieces):
        moved = pltpu.roll(piece.astype(F32), (place * width - start) % 128, 1)
        total = moved if total is None else jnp.where(lane >= place * width, moved, total)
    return total


def side_lanes(from_right, from_left, place, width):
    lane = lanes(64)
    right = pltpu.roll(from_right.astype(F32), (-place * width) % 128, 1)
    left = pltpu.roll(from_left.astype(F32), (128 - width - place * width) % 128, 1)
    side = jnp.where(lane < width, right, jnp.where(lane >= 128 - width, left, 0.0))
    return side.astype(BF)


def tap_sums(taps, spacing, narrow):
    lane = lanes(32)
    before, after = lane >= spacing, lane < 128 - spacing
    sums = []
    for tap in taps:
        left = [pltpu.roll(tap[:32, h : h + 128], spacing, 1) for h in (0, 128)]
        right = [pltpu.roll(tap[64:, h : h + 128], 128 - spacing, 1) for h in (0, 128)]
        sums.append(
            [
                tap[32:64, 128 * h : 128 * h + 128]
                + jnp.where(before, left[h], left[1 - h])
                + jnp.where(after, right[h], right[1 - h])
                for h in range(1 if narrow else 2)
            ]
        )
    return sums


def conv_rows(source, rows, spacing, kernel, narrow):
    taps = []
    for at in rows:
        stacked = jnp.concatenate(
            [source[at - spacing], source[at], source[at + spacing]], axis=0
        )
        taps.append(jnp.dot(kernel, jnp.maximum(stacked, 0), preferred_element_type=F32))
    return tap_sums(taps, spacing, narrow)


def grow(sums, gain, shift, expand):
    hidden = [jnp.maximum(gain * conv + shift, 0.0).astype(BF) for conv in sums]
    grown = []
    for i in range(0, len(hidden), 2):
        both = jnp.dot(
            expand, jnp.concatenate(hidden[i : i + 2], axis=1), preferred_element_type=F32
        )
        grown += [both[:, :128], both[:, 128:]]
    return grown


def block_rows(source, rows, spacing, kernel, gain, shift, expand, narrow=False):
    sums = conv_rows(source, rows, spacing, kernel, narrow)
    grown = grow([conv for row in sums for conv in row], gain, shift, expand)
    if narrow:
        return [source[at, :, :128].astype(F32) + g for at, g in zip(rows, grown)]
    return [
        source[at].astype(F32) + jnp.concatenate(grown[2 * i : 2 * i + 2], axis=1)
        for i, at in enumerate(rows)
    ]


def block_of(layer, spacing_ref, kernel_ref, gain_ref, shift_ref, expand_ref):
    return (
        spacing_ref[layer], kernel_ref[layer], gain_ref[layer], shift_ref[layer], expand_ref[layer]
    )


def pack_rows(rows, odd, sides_ref):
    for g in range(len(rows) // 8):
        pieces = rows[8 * g : 8 * g + 8]
        left, right = pack_strips(pieces, 0, 16), pack_strips(pieces, 112, 16)
        sides_ref[0, g] = jnp.where(odd, left, right).astype(BF)
        sides_ref[1, g] = jnp.where(odd, right, left).astype(BF)


def pack_sides(parity_ref, near_row, far_row, own_ref, sides_ref):
    odd = jnp.broadcast_to(parity_ref[1], (64, 128)) == 1
    rows = [ref[r] for ref in (near_row, own_ref, far_row) for r in range(ref.shape[0])]
    pack_rows(rows, odd, sides_ref)


def fill_wide(wide, parts, odd_col, near_ref, far_ref):
    for ref, count, source, start, block in parts:
        for r in range(count):
            if r % 8 == 0:
                near, far = near_ref[block + r // 8], far_ref[block + r // 8]
                from_left = jnp.where(odd_col, near, far)
                from_right = jnp.where(odd_col, far, near)
            wide[start + r, :, :128] = ref[source + r]
            wide[start + r, :, 128:] = side_lanes(from_right, from_left, r % 8, 16)


def first_blocks(
    scalar_ref, near_row, own_ref, far_row, near_ref, far_ref,
    kernel_ref, gain_ref, shift_ref, expand_ref,
    second_ref, message_ref, wide, middle, turned,
):
    row, col, members = scalar_ref[3], scalar_ref[4], scalar_ref[5]
    weights = (scalar_ref, kernel_ref, gain_ref, shift_ref, expand_ref)
    far_start = 48 * lax.rem(row, 2)
    parts = (
        (near_row, 16, 0, 48 - far_start, 0),
        (own_ref, 32, 0, 16, 2),
        (far_row, 16, 0, far_start, 6),
    )
    fill_wide(wide, parts, lax.rem(col, 2) == 1, near_ref, far_ref)
    lane = lax.broadcasted_iota(jnp.int32, (64, 256), 1)
    inside = (lane < 128) | ((lane < 192) & (col < 7)) | ((lane >= 192) & (col > 0))

    outs = block_rows(wide, [r + 8 for r in range(48)], *block_of(0, *weights))
    for r, out in enumerate(outs):
        alive = inside
        if not 8 <= r < 40:
            number = 32 * row - 8 + r
            alive = inside & (number >= 0) & (number < 1024)
        middle[r] = jnp.where(alive, out, 0.0).astype(BF)
    rows = [r for b in range(16) for r in (b, b + 16)]
    outs = block_rows(middle, [r + 8 for r in rows], *block_of(1, *weights), narrow=True)
    for r, out in zip(rows, outs):
        second_ref[r] = out.astype(BF)
    for b in range(16):
        pair = jnp.concatenate(outs[2 * b : 2 * b + 2], axis=0).astype(BF)
        turned[pl.ds(b, 128, stride=16), :] = jnp.transpose(pair.astype(F32))
    for m in range(4):
        message_ref[lax.bitwise_xor(members, m)] = turned[512 * m : 512 * m + 512].astype(BF)


def average(scalar_ref, second_ref, m0, m1, m2, m3, mean_ref, sides_ref, gathered):
    members = scalar_ref[5]
    for t, ref in enumerate((m0, m1, m2, m3)):
        gathered[lax.bitwise_xor(members, t)] = ref[...]
    mean = []
    for j in range(32):
        blocks = []
        for k in range(4):
            part = gathered[k, 16 * j : 16 * j + 16, :].astype(F32)
            blocks += [part, pltpu.roll(part, 64, 1)]
        mirrored = jnp.transpose(jnp.concatenate(blocks, axis=0))[:64]
        mean.append((0.5 * (second_ref[j].astype(F32) + mirrored)).astype(BF))
        mean_ref[j] = mean[j]
    pack_rows(mean, lax.rem(scalar_ref[4], 2) == 1, sides_ref)


def edge_rows(mean_ref, scalar_ref, near_ref, far_ref, wide):
    for r in range(8):
        wide[r] = jnp.zeros((64, 256), BF)
        wide[24 + r] = jnp.zeros((64, 256), BF)
    parts = ((mean_ref, 8, 0, 8, 0), (mean_ref, 8, 24, 16, 3))
    fill_wide(wide, parts, lax.rem(scalar_ref[4], 2) == 1, near_ref, far_ref)


def last_edges(
    scalar_ref, mean_ref, near_ref, far_ref, kernel_ref, to_far_ref, to_near_ref, wide
):
    spacing, kernel = scalar_ref[2], kernel_ref[2]
    odd = lax.rem(scalar_ref[3], 2) == 1
    edge_rows(mean_ref, scalar_ref, near_ref, far_ref, wide)
    taps = []
    for i in range(8):
        up = jnp.maximum(wide[i + spacing], 0)
        taps.append(jnp.dot(kernel[:, 128:], up, preferred_element_type=F32))
        down = jnp.maximum(wide[24 + i - spacing], 0)
        taps.append(jnp.dot(kernel[:, :64], down, preferred_element_type=F32))
    sums = tap_sums(taps, spacing, True)
    for i in range(8):
        up, down = sums[2 * i][0], sums[2 * i + 1][0]
        to_far_ref[i] = jnp.where(odd, down, up).astype(BF)
        to_near_ref[i] = jnp.where(odd, up, down).astype(BF)


def last_inner(
    scalar_ref, mean_ref, near_ref, far_ref, kernel_ref, gain_ref, shift_ref, expand_ref,
    out_ref, conv_ref, wide,
):
    for at in range(8):
        wide[at] = jnp.zeros((64, 256), BF)
        wide[40 + at] = jnp.zeros((64, 256), BF)
    parts = ((mean_ref, 32, 0, 8, 0),)
    fill_wide(wide, parts, lax.rem(scalar_ref[4], 2) == 1, near_ref, far_ref)
    sums = conv_rows(wide, [r + 8 for r in range(32)], scalar_ref[2], kernel_ref[2], True)
    sums = [row[0] for row in sums]
    for i in range(8):
        conv_ref[i] = sums[i]
        conv_ref[8 + i] = sums[24 + i]
    grown = grow(sums[8:24], gain_ref[2], shift_ref[2], expand_ref[2])
    for i in range(16):
        out_ref[8 + i] = (mean_ref[8 + i].astype(F32) + grown[i]).astype(BF)


def last_outer(
    parity_ref, inner_ref, mean_ref, conv_ref, far_row, near_row, gain_ref, shift_ref, expand_ref,
    out_ref,
):
    odd = jnp.broadcast_to(parity_ref[0], (32, 128)) == 1
    near = [near_row[i].astype(F32) for i in range(8)]
    far = [far_row[i].astype(F32) for i in range(8)]
    sums = [conv_ref[i] + jnp.where(odd, near[i], far[i]) for i in range(8)]
    sums += [conv_ref[8 + i] + jnp.where(odd, far[i], near[i]) for i in range(8)]
    grown = grow(sums, gain_ref[2], shift_ref[2], expand_ref[2])
    out_ref[8:24] = inner_ref[8:24]
    for i in range(16):
        at = i if i < 8 else 16 + i
        out_ref[at] = (mean_ref[at].astype(F32) + grown[i]).astype(BF)


def on_device(contact_map, dilations, conv_weight, conv_gain, conv_shift, out_weight):
    rows, cols = lax.axis_size("row"), lax.axis_size("col")
    row, col = lax.axis_index("row"), lax.axis_index("col")
    mixed = lax.bitwise_xor(lax.rem(row, 4), lax.rem(lax.div(row, 4) + col, 4))
    scalars = jnp.concatenate([dilations, jnp.stack([row, col, mixed]).astype(jnp.int32)])
    parity = jnp.broadcast_to(
        jnp.stack([lax.rem(row, 2), lax.rem(col, 2)]).astype(jnp.int32)[:, None, None], (2, 1, 128)
    )
    near_rows = [(r, r ^ 1) for r in range(rows)]
    far_rows = [(r, r + 1) for r in range(1, rows - 1, 2)]
    far_rows += [(d, r) for r, d in far_rows]
    near_pairs = [(c, c ^ 1) for c in range(cols)]
    far_pairs = [(c, c + 1) for c in range(1, cols - 1, 2)]
    far_pairs += [(d, c) for c, d in far_pairs]

    own = jnp.transpose(lax.optimization_barrier(contact_map), (1, 0, 2))
    odd_row = lax.rem(row, 2)

    def rim(start):
        part = lax.dynamic_slice_in_dim(contact_map, start, 16, 1)
        return jnp.transpose(lax.optimization_barrier(part), (1, 0, 2))

    far_row = lax.ppermute(rim(16 * odd_row), "row", far_rows)
    near_row = lax.ppermute(rim(16 - 16 * odd_row), "row", near_rows)
    sides = call(
        pack_sides,
        jax.ShapeDtypeStruct((2, 8, 64, 128), BF),
        (parity, near_row, far_row, own),
        0,
        [],
        0,
        1 << 20,
    )
    far = lax.ppermute(sides[1], "col", far_pairs)
    near = lax.ppermute(sides[0], "col", near_pairs)
    kernel = jnp.transpose(conv_weight.reshape(3, 3, 3, 32, 64), (0, 2, 3, 1, 4)).reshape(3, 96, 192)
    gain = jnp.broadcast_to(conv_gain[:, :, None], (3, 32, 128))
    shift = jnp.broadcast_to(conv_shift[:, :, None], (3, 32, 128))
    weights = (kernel, gain, shift, out_weight)

    tile = jax.ShapeDtypeStruct((32, 64, 128), BF)
    second, messages = call(
        first_blocks,
        (tile, jax.ShapeDtypeStruct((4, 512, 128), BF)),
        (scalars, near_row, own, far_row, near, far, *weights),
        1,
        [
            pltpu.VMEM((64, 64, 256), BF),
            pltpu.VMEM((48, 64, 256), BF),
            pltpu.VMEM((128 * 16, 128), F32),
        ],
        80 * 256 * 64 * 32 * 20,
        4 << 20,
    )
    received = []
    for t in range(4):
        pairs = []
        for a in range(rows // 4):
            for k in range(4):
                for b in range(cols):
                    pairs.append(((4 * a + k) * cols + b, (4 * b + (k ^ t ^ (a + b) % 4)) * cols + a))
        received.append(lax.ppermute(messages[t], BOTH, pairs))
    mean, sides = call(
        average,
        (tile, jax.ShapeDtypeStruct((2, 4, 64, 128), BF)),
        (scalars, second, *received),
        1,
        [pltpu.VMEM((4, 512, 128), BF)],
        0,
        2 << 20,
    )
    far = lax.ppermute(sides[1], "col", far_pairs)
    near = lax.ppermute(sides[0], "col", near_pairs)
    edge = jax.ShapeDtypeStruct((8, 32, 128), BF)
    to_far, to_near = call(
        last_edges,
        (edge, edge),
        (scalars, mean, near, far, kernel),
        1,
        [pltpu.VMEM((32, 64, 256), BF)],
        16 * 256 * 64 * 96 * 2,
        1 << 19,
    )
    far_row = lax.ppermute(to_far, "row", far_rows)
    near_row = lax.ppermute(to_near, "row", near_rows)
    inner, conv = call(
        last_inner,
        (tile, jax.ShapeDtypeStruct((16, 32, 128), F32)),
        (scalars, mean, near, far, *weights),
        1,
        [pltpu.VMEM((48, 64, 256), BF)],
        32 * 256 * 64 * 32 * 20,
        2 << 20,
    )
    out = call(
        last_outer,
        tile,
        (parity, inner, mean, conv, far_row, near_row, gain, shift, out_weight),
        0,
        [],
        16 * 256 * 64 * 32 * 2,
        2 << 20,
    )
    return jnp.transpose(out, (1, 0, 2))


def solution(mesh):
    return jax.shard_map(
        on_device,
        mesh=mesh,
        in_specs=(P(None, "row", "col"), P(), P(), P(), P(), P()),
        out_specs=P(None, "row", "col"),
        check_vma=False,
    )
```
